512 devices in a mesh: blk: 64 (over y_lo, z, core), grp: 8 (over x, y_hi).
Axes of the slice: x: 4, y: 8 (y_hi: 2, y_lo: 4; y = y_hi * 4 + y_lo), z: 8, core: 2. Of those that a mesh axis runs over, the one named last changes fastest.
Arguments:
- embeddings: bfloat16 [262144, 512], P(('blk', 'grp')), may hold values from -6 to 6
- frame_weight: bfloat16 [262144], P(('blk', 'grp')), may hold values from 0.3984375 to 1.59375
- candidates: int32 [64, 8, 4, 8], P('blk', 'grp'), may hold values from 0 to 511, as said below
- owner: int32 [512], replicated, may hold values from 0 to 7, as said below
Outputs:
- best_score: float32 [262144], P(('blk', 'grp'))
- matches: bfloat16 [64, 8, 8, 2, 128, 128], P('blk', 'grp')
The draws below stay inside these ranges and needn't reach their ends.
Inputs may be any that keep to these rules, and one draw needn't show every extreme that they name: `candidates`: offsets lie in 1..3, row and column blocks in 0..3, videos in 0..511. In each device's list at most 2 videos have one owner; for every blk index some owner gets exactly 2 from every grp device of it. `owner`: every partition owns exactly 64 videos.
All inputs are finite; a program needn't handle non-finite values.
Results may differ from the reference program's by a relative error of at most 0.001.
Values may be sent and summed in bfloat16 or wider, within the bound.
A program may use at most 64 MiB of HBM per device.

```python
import jax
import jax.numpy as jnp
from jax import lax

D = 512
F = 512
ROT = 3
PIECE = 128
CAP = 2
VPG = 64
NC = 8
VIDEOS = 512
FRAMES = 262144
N_BLK = 64
N_GRP = 8


def video_order(key):
    return jax.random.permutation(key, VIDEOS).astype(jnp.int32)


def draw_owner(key, part):
    ordering = video_order(key)
    holders = (jnp.arange(VIDEOS, dtype=jnp.int32) // VPG).astype(jnp.int32)
    return jnp.zeros((VIDEOS,), jnp.int32).at[ordering].set(holders)


def draw_candidates(key, part):
    ordering = video_order(key)
    key = jax.random.fold_in(key, 7)
    keys = jax.random.split(key, 7)
    slots_all = N_GRP * CAP
    favored = jax.random.randint(keys[0], (N_BLK, 1, 1), 0, N_GRP)
    slot_range = jnp.arange(slots_all, dtype=jnp.int32)[None, None, :]
    scores = jax.random.randint(keys[1], (N_BLK, N_GRP, slots_all), 0, 1048576) * slots_all + slot_range
    scores = jnp.where(slot_range // CAP == favored, slot_range - slots_all, scores)
    chosen = jnp.argsort(scores, axis=-1, stable=True)[..., :NC].astype(jnp.int32)
    mixing = jax.random.randint(keys[2], (N_BLK, N_GRP, NC), 0, 1048576) * NC + jnp.arange(NC, dtype=jnp.int32)[None, None, :]
    chosen = jnp.take_along_axis(chosen, jnp.argsort(mixing, axis=-1, stable=True).astype(jnp.int32), axis=-1)
    destination = chosen // CAP
    within = jax.random.randint(keys[3], (N_BLK, N_GRP, NC), 0, VPG)
    video_ids = ordering[destination * VPG + within]
    offsets = jax.random.randint(keys[4], (N_BLK, N_GRP, NC), 1, ROT + 1)
    row_block = jax.random.randint(keys[5], (N_BLK, N_GRP, NC), 0, F // PIECE)
    col_block = jax.random.randint(keys[6], (N_BLK, N_GRP, NC), 0, F // PIECE)
    return jnp.stack([offsets, row_block, col_block, video_ids], axis=2).astype(jnp.int32)


def block_levels(key, shape, cuts, low, largest):
    level, own = 1.0, jax.random.fold_in(key, 6)
    for dim, parts in cuts:
        heights = jnp.exp(jax.random.uniform(jax.random.fold_in(own, dim), (parts,), jnp.float32, low / len(cuts), largest / len(cuts)))
        level = level * jnp.repeat(heights, shape[dim] // parts).reshape([-1 if axis == dim else 1 for axis in range(len(shape))])
    return level


def centred(rng, dims, spread, reach, cuts=(), kind=jnp.bfloat16):
    entries = jax.random.normal(rng, dims, jnp.float32) * spread
    if len(cuts) > 0:
        entries = block_levels(rng, dims, cuts, -0.22, 0.18) * entries
    return jnp.clip(entries, min=-reach, max=reach).astype(kind)


def setup_inputs(seed: int = 0) -> dict:
    seeds = jax.random.split(jax.random.key(seed), 5)
    embeddings = centred(seeds[0], (FRAMES, D), 1.0, 6.0, ((0, 512),))
    frame_weight = jnp.clip(0.3984375 + 1.1953125 * jax.random.uniform(seeds[1], (FRAMES,), jnp.float32) ** block_levels(seeds[1], (FRAMES,), ((0, 512),), -0.2, 0.2), 0.3984375, 1.59375).astype(jnp.bfloat16)
    candidates = draw_candidates(jax.random.fold_in(seeds[4], 71), 0)
    owner = draw_owner(jax.random.fold_in(seeds[4], 71), 0)
    return {"embeddings": embeddings, "frame_weight": frame_weight, "candidates": candidates, "owner": owner}


def smooth_tile(tile_scores, row_weight, col_weight):
    weight_pair = 0.25 * row_weight[:, None] * col_weight[None, :]
    for sweep_index in range(3):
        padded = jnp.pad(tile_scores, 1)
        tile_scores = tile_scores + weight_pair * (padded[:-2, :-2] + padded[2:, 2:])
    return tile_scores


def reference(embeddings, frame_weight, candidates, owner):
    shards = embeddings.reshape(N_BLK, N_GRP, F, D)
    weights = frame_weight.reshape(N_BLK, N_GRP, F)
    scale_factor = D ** -0.5
    video_range = jnp.arange(VIDEOS, dtype=jnp.int32)
    group_range = jnp.arange(N_GRP, dtype=jnp.int32)
    slot_range = jnp.arange(CAP, dtype=jnp.int32)
    list_range = jnp.arange(NC, dtype=jnp.int32)

    def device_work(flat_index):
        blk_index = flat_index // N_GRP
        grp_index = flat_index % N_GRP
        own_rows = shards[blk_index, grp_index]
        row_weight = weights[blk_index, grp_index].astype(jnp.float32)
        listing = candidates[blk_index, grp_index]
        tile_index, row_block, col_block, video_ids = listing[0], listing[1], listing[2], listing[3]
        best_score = jnp.full((F,), -jnp.inf, jnp.float32)
        pieces = jnp.zeros((NC, PIECE, PIECE), jnp.float32)
        for offset in range(1, ROT + 1):
            source = ((blk_index - offset) % N_BLK).astype(jnp.int32)
            other_rows = shards[source, grp_index]
            col_weight = weights[source, grp_index].astype(jnp.float32)
            tile_scores = jnp.dot(own_rows, other_rows.T, preferred_element_type=jnp.float32) * scale_factor
            tile_scores = smooth_tile(tile_scores, row_weight, col_weight)
            best_score = jnp.maximum(best_score, jnp.max(tile_scores, axis=1))

            def cut_piece(row_one, col_one):
                return lax.dynamic_slice(tile_scores, ((row_one * PIECE).astype(jnp.int32), (col_one * PIECE).astype(jnp.int32)), (PIECE, PIECE))

            cut = jax.vmap(cut_piece)(row_block, col_block)
            pieces = jnp.where((tile_index == offset)[:, None, None], cut, pieces)
        pieces_low = pieces.astype(jnp.bfloat16)
        destination = jnp.sum(jnp.where(video_ids[:, None] == video_range[None, :], owner[None, :], 0), axis=1)
        same_owner = (destination[:, None] == destination[None, :]) & (list_range[None, :] < list_range[:, None])
        slot_rank = jnp.sum(same_owner.astype(jnp.int32), axis=1)
        dest_hot = (destination[:, None] == group_range[None, :]).astype(jnp.float32)
        slot_hot = (slot_rank[:, None] == slot_range[None, :]).astype(jnp.float32)
        bucket = jnp.einsum("nd,nc,nxy->dcxy", dest_hot, slot_hot, pieces_low.astype(jnp.float32))
        return best_score, bucket.astype(jnp.bfloat16)

    best_all, bucket_all = lax.map(device_work, jnp.arange(N_BLK * N_GRP, dtype=jnp.int32))
    best_out = best_all.reshape(FRAMES)
    matches = bucket_all.reshape(N_BLK, N_GRP, N_GRP, CAP, PIECE, PIECE).transpose(0, 2, 1, 3, 4, 5)
    return best_out, matches
```

```python
import functools

import jax
import jax.numpy as jnp
from jax import lax
from jax.experimental import pallas as pl
from jax.experimental.pallas import tpu as pltpu
from jax.sharding import PartitionSpec as P

MESH = pl.DeviceIdType.MESH
F = 512
D = 512
PIECE = 128
CAP = 2
ROT = 3
GROUPS = 8
STEP = 65
TALL = 8 * STEP
PAD = 8
CHUNKS = 4
SCALE = D ** (-0.5)


def rotate_left(x, n):
    n %= F
    return x if n == 0 else pltpu.roll(x, F - n, 1)


def four(x):
    return jnp.concatenate([x] * 4, axis=1)


def column_weights(w_ref, slot, acs_ref):
    lane = lax.broadcasted_iota(jnp.int32, (8, 128), 1)
    sub = lax.broadcasted_iota(jnp.int32, (8, F), 0)
    rows = [jnp.broadcast_to(w_ref[slot, c : c + 1, :], (8, 128)) for c in range(4)]
    for k in range(2):
        kept = list(rows)
        if k == 0:
            kept[0] = jnp.where(lane == 0, 0.0, kept[0])
        else:
            kept[3] = jnp.where(lane == 127, 0.0, kept[3])
        x = jnp.concatenate(kept, axis=1)
        for bit in (1, 2, 4):
            x = jnp.where((sub & bit) != 0, rotate_left(x, bit), x)
        for m in range((STEP + 6 + 7) // 8):
            acs_ref[k, 8 * m : 8 * m + 8, :] = rotate_left(x, 8 * m - 3)


def row_weights(w_ref, a_ref):
    for r in range(4):
        wide = jnp.broadcast_to(w_ref[0, r : r + 1, :], (128, 128))
        a_ref[PAD + 128 * r : PAD + 128 * (r + 1), :] = jnp.transpose(wide) * 0.25


def product(r_ref, c_ref, t, s_ref):
    for h in range(2):
        part = lax.dot_general(
            r_ref[...],
            c_ref[t, 256 * h : 256 * (h + 1), :],
            (((1,), (1,)), ((), ())),
            preferred_element_type=jnp.float32,
        )
        for k in range(2):
            s_ref[2 * h + k, PAD : PAD + F, :] = part[:, 128 * k : 128 * (k + 1)]


def smooth(s_ref, a_ref, acs_ref, t_ref, m_ref, t):
    levels, weights = {}, {}

    def level(n, q):
        if (n, q) not in levels:
            if n == 0:
                rows = [s_ref[c, pl.ds(PAD + q, 8, stride=STEP), :] for c in range(4)]
                levels[n, q] = rotate_left(jnp.concatenate(rows, axis=1), q)
            else:
                if q not in weights:
                    a = four(a_ref[pl.ds(PAD + q, 8, stride=STEP), :])
                    weights[q] = (a * acs_ref[0, q + 3 : q + 4, :], a * acs_ref[1, q + 3 : q + 4, :])
                before, after = weights[q]
                levels[n, q] = (
                    level(n - 1, q) + before * level(n - 1, q - 1) + after * level(n - 1, q + 1)
                )
        return levels[n, q]

    for q in range(STEP):
        x = level(3, q)
        widest = jnp.maximum(
            jnp.maximum(x[:, :128], x[:, 128:256]), jnp.maximum(x[:, 256:384], x[:, 384:])
        )
        m_ref[pl.ds(q, 8, stride=STEP), :] = jnp.maximum(m_ref[pl.ds(q, 8, stride=STEP), :], widest)
        x = rotate_left(x, -q)
        for c in range(4):
            t_ref[pl.ds((t * 4 + c) * TALL + q, 8, stride=STEP), :] = x[:, 128 * c : 128 * (c + 1)]


def kernel(
    n_blk,
    emb,
    w_in,
    cand,
    owner,
    out,
    best,
    rows,
    cols,
    wx,
    listing,
    plan,
    s_ref,
    a_ref,
    acs_ref,
    t_ref,
    m_ref,
    bucket,
    top,
    loc,
    e_send,
    e_recv,
    z_send,
    z_recv,
    f_send,
    f_recv,
    y_send,
    w_send,
    w_recv,
    c_sem,
    p_send,
    p_recv,
    b_sem,
):
    b, g = lax.axis_index("blk"), lax.axis_index("grp")
    core = lax.rem(b, 2)
    even, odd = core == 0, core == 1
    home = lax.rem(b + 2 * (1 - core), n_blk)

    def behind(k):
        return (lax.rem(b + k + n_blk, n_blk), g)

    def peer(dx, dy):
        return lax.rem(g // 2 + dx, 4) * 2 + lax.rem(g + dy, 2)

    def remote(src, dst, send, recv, device):
        return pltpu.make_async_remote_copy(
            src_ref=src, dst_ref=dst, send_sem=send, recv_sem=recv, device_id=device, device_id_type=MESH
        )

    barrier = pltpu.get_barrier_semaphore()

    def greet(device):
        pl.semaphore_signal(barrier, inc=1, device_id=device, device_id_type=MESH)

    back = lax.rem(b - 2 * (1 - core) + n_blk, n_blk)
    order = [(0, 1), (2, 1), (1, 1), (3, 1), (2, 0), (1, 0), (3, 0)]

    @pl.when(even)
    def _():
        greet(behind(2))
        greet(behind(1))
        greet(behind(-1))
        greet((back, g))

    @pl.when(odd)
    def _():
        greet(behind(-1))
        greet(behind(-2))
        greet(behind(-3))

    for dx, dy in order:
        greet((back, peer(dx, dy)))

    own_rows = pltpu.make_async_copy(emb, rows, loc.at[0])
    own_cols = pltpu.make_async_copy(emb, cols.at[1], loc.at[0])
    own_list = pltpu.make_async_copy(cand, listing, loc.at[1])

    @pl.when(even)
    def _():
        own_cols.start()

    @pl.when(odd)
    def _():
        own_rows.start()
        own_list.start()

    own_slot = 2 * (1 - core)
    wx[own_slot, 0:4, :] = w_in[...].astype(jnp.float32)

    pl.semaphore_wait(barrier, 11 - core)

    quarter = F // CHUNKS
    to_odd = remote(emb, cols.at[0], e_send.at[0], e_recv.at[1], behind(1))
    to_rows = remote(emb, rows, e_send.at[1], e_recv.at[0], behind(-2))
    to_even = remote(emb, cols.at[0], e_send.at[0], e_recv.at[1], behind(-1))

    def chunk(ref, k):
        return ref.at[pl.ds(k * quarter, quarter)]

    ahead = [
        remote(chunk(emb, k), chunk(cols.at[2], k), z_send.at[k], z_recv.at[k], behind(1))
        for k in range(CHUNKS)
    ]
    passed = [
        remote(chunk(cols.at[2], k), chunk(cols.at[1], k), f_send.at[k], f_recv.at[k], behind(1))
        for k in range(CHUNKS)
    ]
    relay = remote(cols.at[0], cols.at[2], y_send.at[0], e_recv.at[2], behind(2))

    def weight(k, steps, slot):
        return remote(wx.at[own_slot], wx.at[slot], w_send.at[k], w_recv.at[slot], behind(steps))

    w_even = [weight(0, -2, 0), weight(1, 1, 1), weight(2, 3, 3)]
    w_odd = [weight(0, -1, 1), weight(1, 1, 3), weight(2, 2, 2)]
    lists = remote(cand, listing, c_sem.at[0], c_sem.at[1], behind(-2))

    @pl.when(even)
    def _():
        lists.start()
        for copy in w_even:
            copy.start()
        to_rows.start()
        to_odd.start()

    @pl.when(odd)
    def _():
        for copy in w_odd:
            copy.start()
        for copy in ahead:
            copy.start()
        to_even.start()

    s_ref[:, 0:PAD, :] = jnp.zeros((4, PAD, 128), jnp.float32)
    s_ref[:, PAD + F :, :] = jnp.zeros((4, s_ref.shape[1] - PAD - F, 128), jnp.float32)
    a_ref[0:PAD, :] = jnp.zeros((PAD, 128), jnp.float32)
    a_ref[PAD + F :, :] = jnp.zeros((a_ref.shape[0] - PAD - F, 128), jnp.float32)
    m_ref[...] = jnp.full_like(m_ref, -jnp.inf)

    @pl.when(even)
    def _():
        own_cols.wait()
        weight(0, -2, 0).wait_recv()
        lists.wait_recv()

    @pl.when(odd)
    def _():
        own_rows.wait()
        own_list.wait()
        weight(2, 2, 2).wait_recv()

    weight(1, 1, 1).wait_recv()
    weight(1, 1, 3).wait_recv()
    row_weights(wx, a_ref)
    for t in range(ROT):
        column_weights(wx, t + 1, acs_ref.at[t])

    count = listing.shape[1]
    where, slot_of, start_of = [], [], []
    for n in range(count):
        where.append(owner[listing[3, n]])
        start_of.append(
            (jnp.maximum(listing[0, n] - 1, 0) * 4 + listing[2, n]) * STEP + listing[1, n] * (PIECE // 8)
        )
        slot = jnp.int32(0)
        for m in range(n):
            slot = slot + jnp.where(where[m] == where[n], 1, 0)
        slot_of.append(slot)
    for d in range(GROUPS):
        for s in range(CAP):
            start, there = jnp.int32(0), jnp.int32(0)
            for n in range(count):
                here = (where[n] == d) & (slot_of[n] == s)
                start = jnp.where(here, start_of[n], start)
                there = jnp.where(here, 1, there)
            plan[0, d * CAP + s] = start
            plan[1, d * CAP + s] = there

    @pl.when(even)
    def _():
        for k in range(CHUNKS):
            ahead[k].wait_recv()
            passed[k].start()
        to_rows.wait_recv()

    to_even.wait_recv()

    @pl.when(odd)
    def _():
        ahead[CHUNKS - 2].wait_send()
        relay.start()

    def tile(t, carry):
        @pl.when(odd & (t == 1))
        def _():
            for k in range(CHUNKS):
                passed[k].wait_recv()

        @pl.when(odd & (t == 2))
        def _():
            relay.wait_recv()

        product(rows, cols, t, s_ref)
        smooth(s_ref, a_ref, acs_ref.at[t], t_ref, m_ref, t)
        return carry

    lax.fori_loop(0, ROT, tile, 0)

    def fill(d):
        for s in range(CAP):
            piece = t_ref[pl.ds(plan[0, d * CAP + s] * 8, PIECE), :]
            there = jnp.broadcast_to(plan[1, d * CAP + s], (PIECE, PIECE)) > 0
            piece = jnp.where(there, piece * SCALE, 0.0)
            bucket[d, PIECE * s : PIECE * (s + 1), :] = piece.astype(jnp.bfloat16)

    def piece_copy(d):
        return remote(bucket.at[d], out.at[g], p_send.at[d], p_recv.at[g], (home, d))

    for dx, dy in order:
        d = peer(dx, dy)
        fill(d)
        piece_copy(d).start()
    fill(g)
    own_piece = pltpu.make_async_copy(bucket.at[g], out.at[g], loc.at[0])

    @pl.when(even)
    def _():
        piece_copy(g).start()

    @pl.when(odd)
    def _():
        own_piece.start()

    for r in range(4):
        block = jnp.transpose(m_ref[128 * r : 128 * (r + 1), :])
        top[r : r + 1, :] = jnp.max(block, axis=0, keepdims=True) * SCALE
    top_home = remote(top, best, b_sem.at[0], b_sem.at[1], behind(2))
    top_here = pltpu.make_async_copy(top, best, loc.at[1])

    @pl.when(even)
    def _():
        top_home.start()

    @pl.when(odd)
    def _():
        top_here.start()

    @pl.when(even)
    def _():
        for copy in w_even:
            copy.wait_send()
        lists.wait_send()
        to_rows.wait_send()
        to_odd.wait_send()
        for copy in passed:
            copy.wait_send()
        top_home.wait()
        piece_copy(g).wait_send()
        piece_copy(g).wait_recv()

    @pl.when(odd)
    def _():
        for copy in w_odd:
            copy.wait_send()
        for k in range(CHUNKS):
            if k != CHUNKS - 2:
                ahead[k].wait_send()
        to_even.wait_send()
        relay.wait_send()
        top_here.wait()
        own_piece.wait()

    for dx, dy in order:
        d = peer(dx, dy)
        piece_copy(d).wait_send()
        remote(bucket.at[d], out.at[d], p_send.at[d], p_recv.at[d], (home, d)).wait_recv()


def body(n_blk, embeddings, frame_weight, candidates, owner):
    count = candidates.shape[3]
    dma = pltpu.SemaphoreType.DMA
    any_, vmem, smem = (pl.BlockSpec(memory_space=m) for m in (pl.ANY, pltpu.VMEM, pltpu.SMEM))
    out, best = pl.pallas_call(
        functools.partial(kernel, n_blk),
        out_shape=(
            jax.ShapeDtypeStruct((GROUPS, CAP * PIECE, PIECE), jnp.bfloat16),
            jax.ShapeDtypeStruct((4, 128), jnp.float32),
        ),
        in_specs=[any_, vmem, any_, smem],
        out_specs=(any_, any_),
        scratch_shapes=[
            pltpu.VMEM((F, D), jnp.bfloat16),
            pltpu.VMEM((ROT, F, D), jnp.bfloat16),
            pltpu.VMEM((4, 8, 128), jnp.float32),
            pltpu.SMEM((4, count), jnp.int32),
            pltpu.SMEM((2, GROUPS * CAP), jnp.int32),
            pltpu.VMEM((4, TALL + 2 * PAD, 128), jnp.float32),
            pltpu.VMEM((TALL + 2 * PAD, 128), jnp.float32),
            pltpu.VMEM((ROT, 2, (STEP + 6 + 7) // 8 * 8, F), jnp.float32),
            pltpu.VMEM((ROT * 4 * TALL, 128), jnp.float32),
            pltpu.VMEM((TALL, 128), jnp.float32),
            pltpu.VMEM((GROUPS, CAP * PIECE, PIECE), jnp.bfloat16),
            pltpu.VMEM((4, 128), jnp.float32),
            dma((2,)),
            dma((2,)),
            dma((3,)),
            dma((CHUNKS,)),
            dma((CHUNKS,)),
            dma((CHUNKS,)),
            dma((CHUNKS,)),
            dma((1,)),
            dma((3,)),
            dma((4,)),
            dma((2,)),
            dma((GROUPS,)),
            dma((GROUPS,)),
            dma((2,)),
        ],
        compiler_params=pltpu.CompilerParams(
            collective_id=0, has_side_effects=True, vmem_limit_bytes=40 << 20
        ),
        name="window_join",
    )(embeddings, frame_weight.reshape(4, 128), candidates.reshape(4, count), owner)
    return best.reshape(F), out.reshape(1, 1, GROUPS, CAP, PIECE, PIECE)


def solution(mesh):
    return jax.shard_map(
        functools.partial(body, mesh.shape["blk"]),
        mesh=mesh,
        in_specs=(P(("blk", "grp"), None), P(("blk", "grp")), P("blk", "grp", None, None), P()),
        out_specs=(P(("blk", "grp")), P("blk", "grp", None, None, None, None)),
        check_vma=False,
    )
```

```python
import functools

import jax
import jax.numpy as jnp
from jax import lax
from jax.experimental import pallas as pl
from jax.experimental.pallas import tpu as pltpu
from jax.sharding import PartitionSpec as P

MESH = pl.DeviceIdType.MESH
F = 512
D = 512
PIECE = 128
CAP = 2
ROT = 3
GROUPS = 8
STEP = 65
TALL = 8 * STEP
PAD = 8
CHUNKS = 4
SCALE = D ** (-0.5)


def rotate_left(x, n):
    n %= F
    return x if n == 0 else pltpu.roll(x, F - n, 1)


def four(x):
    return jnp.concatenate([x] * 4, axis=1)


def column_weights(w_ref, slot, acs_ref):
    lane = lax.broadcasted_iota(jnp.int32, (8, 128), 1)
    sub = lax.broadcasted_iota(jnp.int32, (8, F), 0)
    rows = [jnp.broadcast_to(w_ref[slot, c : c + 1, :], (8, 128)) for c in range(4)]
    for k in range(2):
        kept = list(rows)
        if k == 0:
            kept[0] = jnp.where(lane == 0, 0.0, kept[0])
        else:
            kept[3] = jnp.where(lane == 127, 0.0, kept[3])
        x = jnp.concatenate(kept, axis=1)
        for bit in (1, 2, 4):
            x = jnp.where((sub & bit) != 0, rotate_left(x, bit), x)
        for m in range((STEP + 6 + 7) // 8):
            acs_ref[k, 8 * m : 8 * m + 8, :] = rotate_left(x, 8 * m - 3)


def row_weights(w_ref, a_ref):
    for r in range(4):
        wide = jnp.broadcast_to(w_ref[0, r : r + 1, :], (128, 128))
        a_ref[PAD + 128 * r : PAD + 128 * (r + 1), :] = jnp.transpose(wide) * 0.25


def product(r_ref, c_ref, t, s_ref):
    for h in range(2):
        part = lax.dot_general(
            r_ref[...],
            c_ref[t, 256 * h : 256 * (h + 1), :],
            (((1,), (1,)), ((), ())),
            preferred_element_type=jnp.float32,
        )
        for k in range(2):
            s_ref[2 * h + k, PAD : PAD + F, :] = part[:, 128 * k : 128 * (k + 1)]


def smooth(s_ref, a_ref, acs_ref, t_ref, m_ref, t):
    levels, weights = {}, {}

    def level(n, q):
        if (n, q) not in levels:
            if n == 0:
                rows = [s_ref[c, pl.ds(PAD + q, 8, stride=STEP), :] for c in range(4)]
                levels[n, q] = rotate_left(jnp.concatenate(rows, axis=1), q)
            else:
                if q not in weights:
                    a = four(a_ref[pl.ds(PAD + q, 8, stride=STEP), :])
                    weights[q] = (a * acs_ref[0, q + 3 : q + 4, :], a * acs_ref[1, q + 3 : q + 4, :])
                before, after = weights[q]
                levels[n, q] = (
                    level(n - 1, q) + before * level(n - 1, q - 1) + after * level(n - 1, q + 1)
                )
        return levels[n, q]

    for q in range(STEP):
        x = level(3, q)
        widest = jnp.maximum(
            jnp.maximum(x[:, :128], x[:, 128:256]), jnp.maximum(x[:, 256:384], x[:, 384:])
        )
        m_ref[pl.ds(q, 8, stride=STEP), :] = jnp.maximum(m_ref[pl.ds(q, 8, stride=STEP), :], widest)
        x = rotate_left(x, -q)
        for c in range(4):
            t_ref[pl.ds((t * 4 + c) * TALL + q, 8, stride=STEP), :] = x[:, 128 * c : 128 * (c + 1)]


def kernel(
    n_blk,
    emb,
    w_in,
    cand,
    owner_in,
    out,
    best,
    owner,
    w_own,
    flood,
    rows,
    cols,
    wx,
    listing,
    plan,
    s_ref,
    a_ref,
    acs_ref,
    t_ref,
    m_ref,
    bucket,
    top,
    loc,
    e_send,
    e_recv,
    z_send,
    z_recv,
    f_send,
    f_recv,
    y_send,
    w_send,
    w_recv,
    c_sem,
    p_send,
    p_recv,
    b_sem,
):
    b, g = lax.axis_index("blk"), lax.axis_index("grp")
    core = lax.rem(b, 2)
    even, odd = core == 0, core == 1
    home = lax.rem(b + 2 * (1 - core), n_blk)

    def behind(k):
        return (lax.rem(b + k + n_blk, n_blk), g)

    def peer(dx, dy):
        return lax.rem(g // 2 + dx, 4) * 2 + lax.rem(g + dy, 2)

    def remote(src, dst, send, recv, device):
        return pltpu.make_async_remote_copy(
            src_ref=src, dst_ref=dst, send_sem=send, recv_sem=recv, device_id=device, device_id_type=MESH
        )

    barrier = pltpu.get_barrier_semaphore()
    order = [(0, 1), (2, 1), (1, 1), (3, 1), (2, 0), (1, 0), (3, 0)]
    per_row = n_blk // 4
    turn = 1 - 2 * lax.rem(g, 2)
    y_lo = b // per_row
    y_down = (lax.rem(b - per_row + n_blk, n_blk), g + jnp.where(y_lo == 0, turn, 0))
    y_up = (lax.rem(b + per_row, n_blk), g + jnp.where(y_lo == 3, turn, 0))

    def greet(device, semaphore=barrier):
        pl.semaphore_signal(semaphore, inc=1, device_id=device, device_id_type=MESH)

    @pl.when(even)
    def _():
        greet(behind(-2))
        greet(behind(1))
        greet(behind(-1))

    @pl.when(odd)
    def _():
        greet(behind(-1))
        greet(behind(-2))
        greet(behind(-3))

    greet((b, peer(1, 0)))
    greet((b, peer(3, 0)))
    greet(y_up)

    own_rows = pltpu.make_async_copy(emb, rows, loc.at[0])
    own_cols = pltpu.make_async_copy(emb, cols.at[1], loc.at[0])
    own_list = pltpu.make_async_copy(cand, listing, loc.at[1])
    own_weights = pltpu.make_async_copy(w_in, w_own, loc.at[2])
    owners = pltpu.make_async_copy(owner_in, owner, loc.at[3])
    own_weights.start()

    @pl.when(even)
    def _():
        own_cols.start()

    @pl.when(odd)
    def _():
        own_rows.start()
        own_list.start()

    owners.start()
    own_slot = 2 * (1 - core)
    pl.semaphore_wait(barrier, 6)

    quarter = F // CHUNKS
    to_odd = remote(emb, cols.at[0], e_send.at[0], e_recv.at[1], behind(1))
    to_rows = remote(emb, rows, e_send.at[1], e_recv.at[0], behind(-2))
    to_even = remote(emb, cols.at[0], e_send.at[0], e_recv.at[1], behind(-1))

    def chunk(ref, k):
        return ref.at[pl.ds(k * quarter, quarter)]

    ahead = [
        remote(chunk(emb, k), chunk(cols.at[2], k), z_send.at[k], z_recv.at[k], behind(1))
        for k in range(CHUNKS)
    ]
    passed = [
        remote(chunk(cols.at[2], k), chunk(cols.at[1], k), f_send.at[k], f_recv.at[k], behind(1))
        for k in range(CHUNKS)
    ]
    relay = remote(cols.at[0], cols.at[2], y_send.at[0], e_recv.at[2], behind(2))

    def weight(k, steps, slot):
        return remote(wx.at[own_slot], wx.at[slot], w_send.at[k], w_recv.at[slot], behind(steps))

    w_even = [weight(0, -2, 0), weight(1, 1, 1), weight(2, 3, 3)]
    w_odd = [weight(0, -1, 1), weight(1, 1, 3), weight(2, 2, 2)]
    lists = remote(cand, listing, c_sem.at[0], c_sem.at[1], behind(-2))

    first = lax.rem(b // 2, 8) == 0
    last = lax.rem(b // 2, 8) == 7

    def send_rows():
        hear(6)
        to_rows.start()
        lists.start()
        w_even[0].start()

    def hear(k):
        pl.semaphore_wait(flood.at[k], 1)

    @pl.when(even)
    def _():
        greet(behind(2), flood.at[6])
        to_odd.start()

    @pl.when(odd)
    def _():
        for copy in ahead:
            copy.start()
        to_even.start()

    greet((b, peer(3, 0)), flood.at[0])
    own_weights.wait()
    wx[own_slot, 0:4, :] = w_own[...].astype(jnp.float32)

    @pl.when(even)
    def _():
        for copy in w_even[1:]:
            copy.start()

    @pl.when(odd)
    def _():
        for copy in w_odd:
            copy.start()

    pl.when(even & jnp.logical_not(first))(send_rows)
    for k in range(4):
        hear(k)
        greet(y_down, flood.at[k + 1])
    hear(4)

    @pl.when(even & jnp.logical_not(first))
    def _():
        greet(behind(-2), flood.at[5])
        hear(5)

    @pl.when(even & first)
    def _():
        hear(5)
        send_rows()
        greet(behind(-2), flood.at[5])

    to_even.wait_recv()

    @pl.when(odd)
    def _():
        ahead[CHUNKS - 2].wait_send()
        relay.start()

    s_ref[:, 0:PAD, :] = jnp.zeros((4, PAD, 128), jnp.float32)
    s_ref[:, PAD + F :, :] = jnp.zeros((4, s_ref.shape[1] - PAD - F, 128), jnp.float32)
    a_ref[0:PAD, :] = jnp.zeros((PAD, 128), jnp.float32)
    a_ref[PAD + F :, :] = jnp.zeros((a_ref.shape[0] - PAD - F, 128), jnp.float32)
    m_ref[...] = jnp.full_like(m_ref, -jnp.inf)

    @pl.when(even)
    def _():
        own_cols.wait()
        weight(0, -2, 0).wait_recv()
        lists.wait_recv()

    @pl.when(odd)
    def _():
        own_rows.wait()
        own_list.wait()
        weight(2, 2, 2).wait_recv()

    weight(1, 1, 1).wait_recv()
    weight(1, 1, 3).wait_recv()
    owners.wait()
    row_weights(wx, a_ref)
    for t in range(ROT):
        column_weights(wx, t + 1, acs_ref.at[t])

    count = listing.shape[1]
    where, slot_of, start_of = [], [], []
    for n in range(count):
        where.append(owner[listing[3, n]])
        start_of.append(
            (jnp.maximum(listing[0, n] - 1, 0) * 4 + listing[2, n]) * STEP + listing[1, n] * (PIECE // 8)
        )
        slot = jnp.int32(0)
        for m in range(n):
            slot = slot + jnp.where(where[m] == where[n], 1, 0)
        slot_of.append(slot)
    for d in range(GROUPS):
        for s in range(CAP):
            start, there = jnp.int32(0), jnp.int32(0)
            for n in range(count):
                here = (where[n] == d) & (slot_of[n] == s)
                start = jnp.where(here, start_of[n], start)
                there = jnp.where(here, 1, there)
            plan[0, d * CAP + s] = start
            plan[1, d * CAP + s] = there

    pl.when(even)(to_rows.wait_recv)

    def tile(t, carry):
        @pl.when(even & (t == 1 + first.astype(jnp.int32)))
        def _():
            for k in range(CHUNKS):
                ahead[k].wait_recv()
                passed[k].start()

        @pl.when(odd & (t == 1))
        def _():
            for k in range(CHUNKS):
                passed[k].wait_recv()

        @pl.when(odd & (t == 2))
        def _():
            relay.wait_recv()

        product(rows, cols, t, s_ref)
        smooth(s_ref, a_ref, acs_ref.at[t], t_ref, m_ref, t)
        return carry

    lax.fori_loop(0, ROT, tile, 0)

    def fill(d):
        for s in range(CAP):
            piece = t_ref[pl.ds(plan[0, d * CAP + s] * 8, PIECE), :]
            there = jnp.broadcast_to(plan[1, d * CAP + s], (PIECE, PIECE)) > 0
            piece = jnp.where(there, piece * SCALE, 0.0)
            bucket[d, PIECE * s : PIECE * (s + 1), :] = piece.astype(jnp.bfloat16)

    def piece_copy(d):
        return remote(bucket.at[d], out.at[g], p_send.at[d], p_recv.at[g], (home, d))

    pl.when(odd & last)(functools.partial(hear, 7))
    for dx, dy in order:
        d = peer(dx, dy)
        fill(d)
        piece_copy(d).start()
    fill(g)
    own_piece = pltpu.make_async_copy(bucket.at[g], out.at[g], loc.at[0])

    @pl.when(even)
    def _():
        piece_copy(g).start()

    @pl.when(odd)
    def _():
        own_piece.start()

    for r in range(4):
        block = jnp.transpose(m_ref[128 * r : 128 * (r + 1), :])
        top[r : r + 1, :] = jnp.max(block, axis=0, keepdims=True) * SCALE
    top_home = remote(top, best, b_sem.at[0], b_sem.at[1], behind(2))
    top_here = pltpu.make_async_copy(top, best, loc.at[1])

    @pl.when(even)
    def _():
        top_home.start()

    @pl.when(odd)
    def _():
        top_here.start()

    for dx, dy in order:
        piece_copy(peer(dx, dy)).wait_send()

    @pl.when(even & last)
    def _():
        greet(behind(1), flood.at[7])

    @pl.when(even)
    def _():
        for copy in w_even:
            copy.wait_send()
        lists.wait_send()
        to_rows.wait_send()
        to_odd.wait_send()
        for copy in passed:
            copy.wait_send()
        top_home.wait()
        piece_copy(g).wait_send()
        piece_copy(g).wait_recv()

    @pl.when(odd)
    def _():
        for copy in w_odd:
            copy.wait_send()
        for k in range(CHUNKS):
            if k != CHUNKS - 2:
                ahead[k].wait_send()
        to_even.wait_send()
        relay.wait_send()
        top_here.wait()
        own_piece.wait()

    for dx, dy in order:
        d = peer(dx, dy)
        remote(bucket.at[d], out.at[d], p_send.at[d], p_recv.at[d], (home, d)).wait_recv()


def body(n_blk, embeddings, frame_weight, candidates, owner):
    count = candidates.shape[3]
    dma = pltpu.SemaphoreType.DMA
    hbm, vmem = (pl.BlockSpec(memory_space=m) for m in (pltpu.HBM, pltpu.VMEM))
    out, best = pl.pallas_call(
        functools.partial(kernel, n_blk),
        out_shape=(
            jax.ShapeDtypeStruct((GROUPS, CAP * PIECE, PIECE), jnp.bfloat16),
            jax.ShapeDtypeStruct((4, 128), jnp.float32),
        ),
        in_specs=[hbm] * 4,
        out_specs=(vmem, vmem),
        scratch_shapes=[
            pltpu.SMEM(owner.shape, jnp.int32),
            pltpu.VMEM((4, 128), jnp.bfloat16),
            pltpu.SemaphoreType.REGULAR((8,)),
            pltpu.VMEM((F, D), jnp.bfloat16),
            pltpu.VMEM((ROT, F, D), jnp.bfloat16),
            pltpu.VMEM((4, 8, 128), jnp.float32),
            pltpu.SMEM((4, count), jnp.int32),
            pltpu.SMEM((2, GROUPS * CAP), jnp.int32),
            pltpu.VMEM((4, TALL + 2 * PAD, 128), jnp.float32),
            pltpu.VMEM((TALL + 2 * PAD, 128), jnp.float32),
            pltpu.VMEM((ROT, 2, (STEP + 6 + 7) // 8 * 8, F), jnp.float32),
            pltpu.VMEM((ROT * 4 * TALL, 128), jnp.float32),
            pltpu.VMEM((TALL, 128), jnp.float32),
            pltpu.VMEM((GROUPS, CAP * PIECE, PIECE), jnp.bfloat16),
            pltpu.VMEM((4, 128), jnp.float32),
            dma((4,)),
            dma((2,)),
            dma((3,)),
            dma((CHUNKS,)),
            dma((CHUNKS,)),
            dma((CHUNKS,)),
            dma((CHUNKS,)),
            dma((1,)),
            dma((3,)),
            dma((4,)),
            dma((2,)),
            dma((GROUPS,)),
            dma((GROUPS,)),
            dma((2,)),
        ],
        compiler_params=pltpu.CompilerParams(
            collective_id=0, has_side_effects=True, vmem_limit_bytes=40 << 20
        ),
        name="window_join",
    )(*(
        pltpu.with_memory_space_constraint(x, pltpu.HBM)
        for x in (embeddings, frame_weight.reshape(4, 128), candidates.reshape(4, count), owner)
    ))
    return best.reshape(F), out.reshape(1, 1, GROUPS, CAP, PIECE, PIECE)


def solution(mesh):
    return jax.shard_map(
        functools.partial(body, mesh.shape["blk"]),
        mesh=mesh,
        in_specs=(P(("blk", "grp"), None), P(("blk", "grp")), P("blk", "grp", None, None), P()),
        out_specs=(P(("blk", "grp")), P("blk", "grp", None, None, None, None)),
        check_vma=False,
    )
```

```python
import functools

import jax
import jax.numpy as jnp
from jax import lax
from jax.experimental import pallas as pl
from jax.experimental.pallas import tpu as pltpu
from jax.sharding import PartitionSpec as P

MESH = pl.DeviceIdType.MESH
F = 512
D = 512
PIECE = 128
CAP = 2
ROT = 3
GROUPS = 8
STEP = 65
HALF_STEP = 33
PAD = 16
TALL = PAD + 8 * STEP
CHUNKS = 4
SCALE = D ** (-0.5)


def rotate_left(x, n):
    n %= F
    return x if n == 0 else pltpu.roll(x, F - n, 1)


def four(x):
    return jnp.concatenate([x] * 4, axis=1)


def column_weights(w_ref, slot, acs_ref):
    lane = lax.broadcasted_iota(jnp.int32, (8, 128), 1)
    sub = lax.broadcasted_iota(jnp.int32, (8, F), 0)
    rows = [jnp.broadcast_to(w_ref[slot, c : c + 1, :], (8, 128)) for c in range(4)]
    for k in range(2):
        kept = list(rows)
        if k == 0:
            kept[0] = jnp.where(lane == 0, 0.0, kept[0])
        else:
            kept[3] = jnp.where(lane == 127, 0.0, kept[3])
        x = jnp.concatenate(kept, axis=1)
        for bit in (1, 2, 4):
            x = jnp.where((sub & bit) != 0, rotate_left(x, bit), x)
        for m in range((STEP + 6 + 7) // 8):
            acs_ref[k, 8 * m : 8 * m + 8, :] = rotate_left(x, 8 * m - 3)


def row_weights(w_ref, a_ref):
    for r in range(4):
        wide = jnp.broadcast_to(w_ref[0, r : r + 1, :], (128, 128))
        a_ref[PAD + 128 * r : PAD + 128 * (r + 1), :] = jnp.transpose(wide) * 0.25


def product(r_ref, c_ref, t, s_ref, row, count):
    for h in range(2):
        part = lax.dot_general(
            r_ref[pl.ds(row, count), :],
            c_ref[t, 256 * h : 256 * (h + 1), :],
            (((1,), (1,)), ((), ())),
            preferred_element_type=jnp.float32,
        )
        for k in range(2):
            s_ref[t, 2 * h + k, pl.ds(PAD + row, count), :] = part[:, 128 * k : 128 * (k + 1)]


def smooth(s_ref, a_ref, acs_ref, t_ref, m_ref, t, row, step):
    levels, weights = {}, {}

    def level(n, q):
        if (n, q) not in levels:
            if n == 0:
                rows = [s_ref[t, c, pl.ds(PAD + row + q, 8, stride=step), :] for c in range(4)]
                levels[n, q] = rotate_left(jnp.concatenate(rows, axis=1), q)
            else:
                if q not in weights:
                    a = four(a_ref[pl.ds(PAD + row + q, 8, stride=step), :])
                    weights[q] = (
                        a * acs_ref[t, 0, q + 3 : q + 4, :],
                        a * acs_ref[t, 1, q + 3 : q + 4, :],
                    )
                before, after = weights[q]
                levels[n, q] = (
                    level(n - 1, q) + before * level(n - 1, q - 1) + after * level(n - 1, q + 1)
                )
        return levels[n, q]

    for q in range(step):
        x = level(3, q)
        widest = jnp.maximum(
            jnp.maximum(x[:, :128], x[:, 128:256]), jnp.maximum(x[:, 256:384], x[:, 384:])
        )
        where = pl.ds(PAD + row + q, 8, stride=step)
        m_ref[where, :] = jnp.maximum(m_ref[where, :], widest)
        x = rotate_left(x, -q)
        for c in range(4):
            where = pl.ds((t * 4 + c) * TALL + PAD + row + q, 8, stride=step)
            t_ref[where, :] = x[:, 128 * c : 128 * (c + 1)]


def kernel(
    n_blk,
    emb,
    w_in,
    cand,
    owner_in,
    out,
    best,
    owner,
    w_own,
    flood,
    rows,
    cols,
    wx,
    listing,
    plan,
    s_ref,
    a_ref,
    acs_ref,
    t_ref,
    m_ref,
    bucket,
    top,
    loc,
    e_send,
    e_recv,
    r_send,
    r_recv,
    z_send,
    z_recv,
    f_send,
    f_recv,
    y_send,
    w_send,
    w_recv,
    c_sem,
    p_send,
    p_recv,
    b_sem,
):
    b, g = lax.axis_index("blk"), lax.axis_index("grp")
    core = lax.rem(b, 2)
    even, odd = core == 0, core == 1
    home = lax.rem(b + 2 * (1 - core), n_blk)

    def behind(k):
        return (lax.rem(b + k + n_blk, n_blk), g)

    def peer(dx, dy):
        return lax.rem(g // 2 + dx, 4) * 2 + lax.rem(g + dy, 2)

    def remote(src, dst, send, recv, device):
        return pltpu.make_async_remote_copy(
            src_ref=src, dst_ref=dst, send_sem=send, recv_sem=recv, device_id=device, device_id_type=MESH
        )

    barrier = pltpu.get_barrier_semaphore()
    order = [(0, 1), (2, 1), (1, 1), (3, 1), (2, 0), (1, 0), (3, 0)]
    per_row = n_blk // 4
    turn = 1 - 2 * lax.rem(g, 2)
    y_lo = b // per_row
    y_down = (lax.rem(b - per_row + n_blk, n_blk), g + jnp.where(y_lo == 0, turn, 0))
    y_up = (lax.rem(b + per_row, n_blk), g + jnp.where(y_lo == 3, turn, 0))

    def greet(device, semaphore=barrier):
        pl.semaphore_signal(semaphore, inc=1, device_id=device, device_id_type=MESH)

    @pl.when(even)
    def _():
        greet(behind(-2))
        greet(behind(1))
        greet(behind(-1))

    @pl.when(odd)
    def _():
        greet(behind(-1))
        greet(behind(-2))
        greet(behind(-3))

    greet((b, peer(1, 0)))
    greet((b, peer(3, 0)))
    greet(y_up)

    own_rows = pltpu.make_async_copy(emb, rows, loc.at[0])
    own_cols = pltpu.make_async_copy(emb, cols.at[1], loc.at[0])
    own_list = pltpu.make_async_copy(cand, listing, loc.at[1])
    own_weights = pltpu.make_async_copy(w_in, w_own, loc.at[2])
    owners = pltpu.make_async_copy(owner_in, owner, loc.at[3])
    own_weights.start()

    @pl.when(even)
    def _():
        own_cols.start()

    @pl.when(odd)
    def _():
        own_rows.start()
        own_list.start()

    owners.start()
    own_slot = 2 * (1 - core)
    own_weights.wait()
    wx[own_slot, 0:4, :] = w_own[...].astype(jnp.float32)
    pl.semaphore_wait(barrier, 6)

    quarter = F // CHUNKS
    to_odd = remote(emb, cols.at[0], e_send.at[0], e_recv.at[1], behind(1))
    half = F // 2
    to_rows = [
        remote(
            emb.at[pl.ds(k * half, half)], rows.at[pl.ds(k * half, half)], r_send.at[k], r_recv.at[k], behind(-2)
        )
        for k in range(2)
    ]
    to_even = remote(emb, cols.at[0], e_send.at[0], e_recv.at[1], behind(-1))

    def chunk(ref, k):
        return ref.at[pl.ds(k * quarter, quarter)]

    ahead = [
        remote(chunk(emb, k), chunk(cols.at[2], k), z_send.at[k], z_recv.at[k], behind(1))
        for k in range(CHUNKS)
    ]
    passed = [
        remote(chunk(cols.at[2], k), chunk(cols.at[1], k), f_send.at[k], f_recv.at[k], behind(1))
        for k in range(CHUNKS)
    ]
    relay = remote(cols.at[0], cols.at[2], y_send.at[0], e_recv.at[2], behind(2))

    def weight(k, steps, slot):
        return remote(wx.at[own_slot], wx.at[slot], w_send.at[k], w_recv.at[slot], behind(steps))

    w_even = [weight(0, -2, 0), weight(1, 1, 1), weight(2, 3, 3)]
    w_odd = [weight(0, -1, 1), weight(1, 1, 3), weight(2, 2, 2)]
    lists = remote(cand, listing, c_sem.at[0], c_sem.at[1], behind(-2))

    first = lax.rem(b // 2, 8) == 0
    last = lax.rem(b // 2, 8) == 7

    def send_rows():
        hear(6)
        w_even[0].start()
        lists.start()
        for copy in to_rows:
            copy.start()

    def hear(k):
        pl.semaphore_wait(flood.at[k], 1)

    @pl.when(even)
    def _():
        greet(behind(2), flood.at[6])
        for copy in w_even[1:]:
            copy.start()
        to_odd.start()

    @pl.when(odd)
    def _():
        for copy in w_odd:
            copy.start()
        to_even.start()
        for copy in ahead:
            copy.start()

    greet((b, peer(3, 0)), flood.at[0])
    pl.when(even & jnp.logical_not(first))(send_rows)
    for k in range(4):
        hear(k)
        greet(y_down, flood.at[k + 1])

    def tell_behind():
        hear(4)
        greet(behind(-2), flood.at[5])

    @pl.when(even & first)
    def _():
        send_rows()
        tell_behind()

    to_even.wait_recv()

    @pl.when(odd)
    def _():
        ahead[CHUNKS - 2].wait_send()
        relay.start()

    s_ref[:, :, 0:PAD, :] = jnp.zeros((ROT, 4, PAD, 128), jnp.float32)
    s_ref[:, :, PAD + F :, :] = jnp.zeros((ROT, 4, s_ref.shape[2] - PAD - F, 128), jnp.float32)
    a_ref[0:PAD, :] = jnp.zeros((PAD, 128), jnp.float32)
    a_ref[PAD + F :, :] = jnp.zeros((a_ref.shape[0] - PAD - F, 128), jnp.float32)
    m_ref[...] = jnp.full_like(m_ref, -jnp.inf)

    @pl.when(even)
    def _():
        own_cols.wait()
        weight(0, -2, 0).wait_recv()
        lists.wait_recv()

    @pl.when(odd)
    def _():
        own_rows.wait()
        own_list.wait()
        weight(2, 2, 2).wait_recv()

    weight(1, 1, 1).wait_recv()
    weight(1, 1, 3).wait_recv()
    owners.wait()
    row_weights(wx, a_ref)
    for t in range(ROT):
        column_weights(wx, t + 1, acs_ref.at[t])

    count = listing.shape[1]
    where, slot_of, start_of = [], [], []
    for n in range(count):
        where.append(owner[listing[3, n]])
        start_of.append(
            (jnp.maximum(listing[0, n] - 1, 0) * 4 + listing[2, n]) * (TALL // 8) + PAD // 8 + listing[1, n] * (PIECE // 8)
        )
        slot = jnp.int32(0)
        for m in range(n):
            slot = slot + jnp.where(where[m] == where[n], 1, 0)
        slot_of.append(slot)
    for d in range(GROUPS):
        for s in range(CAP):
            start, there = jnp.int32(0), jnp.int32(0)
            for n in range(count):
                here = (where[n] == d) & (slot_of[n] == s)
                start = jnp.where(here, start_of[n], start)
                there = jnp.where(here, 1, there)
            plan[0, d * CAP + s] = start
            plan[1, d * CAP + s] = there

    def half_tile(k, carry):
        h = jnp.where(first, jnp.where(k < 4, k // 2, k - 4), k // 3)
        t = jnp.where(first, jnp.where(k < 4, lax.rem(k, 2), 2), lax.rem(k, 3))

        @pl.when((t == 0) & (h == 0))
        def _():
            to_rows[0].wait_recv()

        @pl.when((t == 0) & (h == 1))
        def _():
            to_rows[1].wait_recv()

        @pl.when((t == 2) & (h == 0))
        def _():
            for c in range(CHUNKS):
                ahead[c].wait_recv()
                passed[c].start()

        pl.when((k == 2) & jnp.logical_not(first))(tell_behind)
        pl.when(k == 4)(functools.partial(hear, 5))
        product(rows, cols, t, s_ref, h * half, half)
        smooth(s_ref, a_ref, acs_ref, t_ref, m_ref, t, h * (F - 8 * HALF_STEP + 12) - 12, HALF_STEP)
        return carry

    def tile(t, carry):
        @pl.when(t == 1)
        def _():
            for c in range(CHUNKS):
                passed[c].wait_recv()

        @pl.when(t == 2)
        def _():
            hear(4)
            relay.wait_recv()

        product(rows, cols, t, s_ref, 0, F)
        smooth(s_ref, a_ref, acs_ref, t_ref, m_ref, t, 0, STEP)
        return carry

    @pl.when(even)
    def _():
        lax.fori_loop(0, 2 * ROT, half_tile, 0)

    @pl.when(odd)
    def _():
        lax.fori_loop(0, ROT, tile, 0)

    def fill(d):
        for s in range(CAP):
            piece = t_ref[pl.ds(plan[0, d * CAP + s] * 8, PIECE), :]
            there = jnp.broadcast_to(plan[1, d * CAP + s], (PIECE, PIECE)) > 0
            piece = jnp.where(there, piece * SCALE, 0.0)
            bucket[d, PIECE * s : PIECE * (s + 1), :] = piece.astype(jnp.bfloat16)

    def piece_copy(d):
        return remote(bucket.at[d], out.at[g], p_send.at[d], p_recv.at[g], (home, d))

    pl.when(odd & last)(functools.partial(hear, 7))
    for dx, dy in order:
        d = peer(dx, dy)
        fill(d)
        piece_copy(d).start()
    fill(g)
    own_piece = pltpu.make_async_copy(bucket.at[g], out.at[g], loc.at[0])

    @pl.when(even)
    def _():
        piece_copy(g).start()

    @pl.when(odd)
    def _():
        own_piece.start()

    for r in range(4):
        block = jnp.transpose(m_ref[PAD + 128 * r : PAD + 128 * (r + 1), :])
        top[r : r + 1, :] = jnp.max(block, axis=0, keepdims=True) * SCALE
    top_home = remote(top, best, b_sem.at[0], b_sem.at[1], behind(2))
    top_here = pltpu.make_async_copy(top, best, loc.at[1])

    @pl.when(even)
    def _():
        top_home.start()

    @pl.when(odd)
    def _():
        top_here.start()

    for dx, dy in order:
        piece_copy(peer(dx, dy)).wait_send()

    @pl.when(even & last)
    def _():
        greet(behind(1), flood.at[7])

    @pl.when(even)
    def _():
        for copy in w_even:
            copy.wait_send()
        lists.wait_send()
        for copy in to_rows:
            copy.wait_send()
        to_odd.wait_send()
        for copy in passed:
            copy.wait_send()
        top_home.wait()
        piece_copy(g).wait_send()
        piece_copy(g).wait_recv()

    @pl.when(odd)
    def _():
        for copy in w_odd:
            copy.wait_send()
        for k in range(CHUNKS):
            if k != CHUNKS - 2:
                ahead[k].wait_send()
        to_even.wait_send()
        relay.wait_send()
        top_here.wait()
        own_piece.wait()

    for dx, dy in order:
        d = peer(dx, dy)
        remote(bucket.at[d], out.at[d], p_send.at[d], p_recv.at[d], (home, d)).wait_recv()


def settle(out_in, best_in, out, best, sems):
    copies = [
        pltpu.make_async_copy(out_in, out, sems.at[0]),
        pltpu.make_async_copy(best_in, best, sems.at[1]),
    ]
    for copy in copies:
        copy.start()
    for copy in copies:
        copy.wait()


def body(n_blk, embeddings, frame_weight, candidates, owner):
    count = candidates.shape[3]
    dma = pltpu.SemaphoreType.DMA
    hbm, vmem = (pl.BlockSpec(memory_space=m) for m in (pltpu.HBM, pltpu.VMEM))
    out, best = pl.pallas_call(
        functools.partial(kernel, n_blk),
        out_shape=(
            jax.ShapeDtypeStruct((GROUPS, CAP * PIECE, PIECE), jnp.bfloat16),
            jax.ShapeDtypeStruct((4, 128), jnp.float32),
        ),
        in_specs=[hbm] * 4,
        out_specs=(vmem, vmem),
        scratch_shapes=[
            pltpu.SMEM(owner.shape, jnp.int32),
            pltpu.VMEM((4, 128), jnp.bfloat16),
            pltpu.SemaphoreType.REGULAR((8,)),
            pltpu.VMEM((F, D), jnp.bfloat16),
            pltpu.VMEM((ROT, F, D), jnp.bfloat16),
            pltpu.VMEM((4, 8, 128), jnp.float32),
            pltpu.SMEM((4, count), jnp.int32),
            pltpu.SMEM((2, GROUPS * CAP), jnp.int32),
            pltpu.VMEM((ROT, 4, TALL + PAD, 128), jnp.float32),
            pltpu.VMEM((TALL + PAD, 128), jnp.float32),
            pltpu.VMEM((ROT, 2, (STEP + 6 + 7) // 8 * 8, F), jnp.float32),
            pltpu.VMEM((ROT * 4 * TALL, 128), jnp.float32),
            pltpu.VMEM((TALL, 128), jnp.float32),
            pltpu.VMEM((GROUPS, CAP * PIECE, PIECE), jnp.bfloat16),
            pltpu.VMEM((4, 128), jnp.float32),
            dma((4,)),
            dma((1,)),
            dma((3,)),
            dma((2,)),
            dma((2,)),
            dma((CHUNKS,)),
            dma((CHUNKS,)),
            dma((CHUNKS,)),
            dma((CHUNKS,)),
            dma((1,)),
            dma((3,)),
            dma((4,)),
            dma((2,)),
            dma((GROUPS,)),
            dma((GROUPS,)),
            dma((2,)),
        ],
        compiler_params=pltpu.CompilerParams(
            collective_id=0, has_side_effects=True, vmem_limit_bytes=40 << 20
        ),
        name="window_join",
    )(*(
        pltpu.with_memory_space_constraint(x, pltpu.HBM)
        for x in (embeddings, frame_weight.reshape(4, 128), candidates.reshape(4, count), owner)
    ))
    out, best = pl.pallas_call(
        settle,
        out_shape=(
            jax.ShapeDtypeStruct(out.shape, out.dtype),
            jax.ShapeDtypeStruct(best.shape, best.dtype),
        ),
        in_specs=[vmem, vmem],
        out_specs=(hbm, hbm),
        scratch_shapes=[dma((2,))],
        name="settle",
    )(*(pltpu.with_memory_space_constraint(x, pltpu.VMEM) for x in (out, best)))
    return best.reshape(F), out.reshape(1, 1, GROUPS, CAP, PIECE, PIECE)


def solution(mesh):
    return jax.shard_map(
        functools.partial(body, mesh.shape["blk"]),
        mesh=mesh,
        in_specs=(P(("blk", "grp"), None), P(("blk", "grp")), P("blk", "grp", None, None), P()),
        out_specs=(P(("blk", "grp")), P("blk", "grp", None, None, None, None)),
        check_vma=False,
    )
```

```python
import functools

import jax
import jax.numpy as jnp
from jax import lax
from jax.experimental import pallas as pl
from jax.experimental.pallas import tpu as pltpu
from jax.sharding import PartitionSpec as P

MESH = pl.DeviceIdType.MESH
F = 512
D = 512
PIECE = 128
CAP = 2
ROT = 3
GROUPS = 8
STEP = 65
HALF_STEP = 33
PAD = 16
TALL = PAD + 8 * STEP
CHUNKS = 4
SCALE = D ** (-0.5)


def rotate_left(x, n):
    n %= F
    return x if n == 0 else pltpu.roll(x, F - n, 1)


def four(x):
    return jnp.concatenate([x] * 4, axis=1)


def column_weights(w_ref, slot, acs_ref):
    lane = lax.broadcasted_iota(jnp.int32, (8, 128), 1)
    sub = lax.broadcasted_iota(jnp.int32, (8, F), 0)
    rows = [jnp.broadcast_to(w_ref[slot, c : c + 1, :], (8, 128)) for c in range(4)]
    for k in range(2):
        kept = list(rows)
        if k == 0:
            kept[0] = jnp.where(lane == 0, 0.0, kept[0])
        else:
            kept[3] = jnp.where(lane == 127, 0.0, kept[3])
        x = jnp.concatenate(kept, axis=1)
        for bit in (1, 2, 4):
            x = jnp.where((sub & bit) != 0, rotate_left(x, bit), x)
        for m in range((STEP + 6 + 7) // 8):
            acs_ref[k, 8 * m : 8 * m + 8, :] = rotate_left(x, 8 * m - 3)


def row_weights(w_ref, a_ref):
    for r in range(4):
        wide = jnp.broadcast_to(w_ref[0, r : r + 1, :], (128, 128))
        a_ref[PAD + 128 * r : PAD + 128 * (r + 1), :] = jnp.transpose(wide) * 0.25


def product(r_ref, c_ref, t, s_ref, row, count):
    for h in range(2):
        part = lax.dot_general(
            r_ref[pl.ds(row, count), :],
            c_ref[t, 256 * h : 256 * (h + 1), :],
            (((1,), (1,)), ((), ())),
            preferred_element_type=jnp.float32,
        )
        for k in range(2):
            s_ref[t, 2 * h + k, pl.ds(PAD + row, count), :] = part[:, 128 * k : 128 * (k + 1)]


def smooth(s_ref, a_ref, acs_ref, t_ref, m_ref, t, row, step):
    levels, weights = {}, {}

    def level(n, q):
        if (n, q) not in levels:
            if n == 0:
                rows = [s_ref[t, c, pl.ds(PAD + row + q, 8, stride=step), :] for c in range(4)]
                levels[n, q] = rotate_left(jnp.concatenate(rows, axis=1), q)
            else:
                if q not in weights:
                    a = four(a_ref[pl.ds(PAD + row + q, 8, stride=step), :])
                    weights[q] = (
                        a * acs_ref[t, 0, q + 3 : q + 4, :],
                        a * acs_ref[t, 1, q + 3 : q + 4, :],
                    )
                before, after = weights[q]
                levels[n, q] = (
                    level(n - 1, q) + before * level(n - 1, q - 1) + after * level(n - 1, q + 1)
                )
        return levels[n, q]

    for q in range(step):
        x = level(3, q)
        widest = jnp.maximum(
            jnp.maximum(x[:, :128], x[:, 128:256]), jnp.maximum(x[:, 256:384], x[:, 384:])
        )
        where = pl.ds(PAD + row + q, 8, stride=step)
        m_ref[where, :] = jnp.maximum(m_ref[where, :], widest)
        x = rotate_left(x, -q)
        for c in range(4):
            where = pl.ds((t * 4 + c) * TALL + PAD + row + q, 8, stride=step)
            t_ref[where, :] = x[:, 128 * c : 128 * (c + 1)]


def kernel(
    n_blk,
    emb,
    w_in,
    cand,
    owner_in,
    out,
    best,
    owner,
    w_own,
    flood,
    rows,
    cols,
    wx,
    listing,
    plan,
    s_ref,
    a_ref,
    acs_ref,
    t_ref,
    m_ref,
    bucket,
    top,
    loc,
    e_send,
    e_recv,
    r_send,
    r_recv,
    z_send,
    z_recv,
    f_send,
    f_recv,
    y_send,
    w_send,
    w_recv,
    c_sem,
    p_send,
    p_recv,
    b_sem,
):
    b, g = lax.axis_index("blk"), lax.axis_index("grp")
    core = lax.rem(b, 2)
    even, odd = core == 0, core == 1
    home = lax.rem(b + 2 * (1 - core), n_blk)

    def behind(k):
        return (lax.rem(b + k + n_blk, n_blk), g)

    def peer(dx, dy):
        return lax.rem(g // 2 + dx, 4) * 2 + lax.rem(g + dy, 2)

    def remote(src, dst, send, recv, device):
        return pltpu.make_async_remote_copy(
            src_ref=src, dst_ref=dst, send_sem=send, recv_sem=recv, device_id=device, device_id_type=MESH
        )

    barrier = pltpu.get_barrier_semaphore()
    per_row = n_blk // 4
    turn = 1 - 2 * lax.rem(g, 2)
    y_lo = b // per_row
    y_down = (lax.rem(b - per_row + n_blk, n_blk), g + jnp.where(y_lo == 0, turn, 0))
    y_up = (lax.rem(b + per_row, n_blk), g + jnp.where(y_lo == 3, turn, 0))

    def greet(device, semaphore=barrier):
        pl.semaphore_signal(semaphore, inc=1, device_id=device, device_id_type=MESH)

    @pl.when(even)
    def _():
        greet(behind(-2))
        greet(behind(1))
        greet(behind(-1))

    @pl.when(odd)
    def _():
        greet(behind(-1))
        greet(behind(-2))
        greet(behind(-3))

    greet((b, peer(1, 0)))
    greet((b, peer(3, 0)))
    greet(y_up)
    own_weights = pltpu.make_async_copy(w_in, w_own, loc.at[2])
    own_weights.start()

    own_rows = pltpu.make_async_copy(emb, rows, loc.at[0])
    own_cols = pltpu.make_async_copy(emb, cols.at[1], loc.at[0])
    own_list = pltpu.make_async_copy(cand, listing, loc.at[1])
    owners = pltpu.make_async_copy(owner_in, owner, loc.at[3])

    own_slot = 2 * (1 - core)
    pl.semaphore_wait(barrier, 6)

    quarter = F // CHUNKS
    to_odd = remote(emb, cols.at[0], e_send.at[0], e_recv.at[1], behind(1))
    half = F // 2
    to_rows = [
        remote(
            emb.at[pl.ds(k * half, half)], rows.at[pl.ds(k * half, half)], r_send.at[k], r_recv.at[k], behind(-2)
        )
        for k in range(2)
    ]
    to_even = remote(emb, cols.at[0], e_send.at[0], e_recv.at[1], behind(-1))

    def chunk(ref, k):
        return ref.at[pl.ds(k * quarter, quarter)]

    ahead = [
        remote(chunk(emb, k), chunk(cols.at[2], k), z_send.at[k], z_recv.at[k], behind(1))
        for k in range(CHUNKS)
    ]
    passed = [
        remote(chunk(cols.at[2], k), chunk(cols.at[1], k), f_send.at[k], f_recv.at[k], behind(1))
        for k in range(CHUNKS)
    ]
    relay = remote(cols.at[0], cols.at[2], y_send.at[0], e_recv.at[2], behind(2))

    def weight(k, steps, slot):
        return remote(wx.at[own_slot], wx.at[slot], w_send.at[k], w_recv.at[slot], behind(steps))

    w_even = [weight(0, -2, 0), weight(1, 1, 1), weight(2, 3, 3)]
    w_odd = [weight(0, -1, 1), weight(1, 1, 3), weight(2, 2, 2)]
    lists = remote(cand, listing, c_sem.at[0], c_sem.at[1], behind(-2))

    first = lax.rem(b // 2, 8) == 0
    last = lax.rem(b // 2, 8) == 7

    def send_rows():
        hear(6)
        w_even[0].start()
        lists.start()
        for copy in to_rows:
            copy.start()

    def hear(k):
        pl.semaphore_wait(flood.at[k], 1)

    @pl.when(even)
    def _():
        greet(behind(2), flood.at[6])
        to_odd.start()

    @pl.when(odd)
    def _():
        ahead[0].start()
        to_even.start()

    greet((b, peer(3, 0)), flood.at[0])

    @pl.when(even)
    def _():
        own_cols.start()

    @pl.when(odd)
    def _():
        own_rows.start()
        own_list.start()

    owners.start()
    own_weights.wait()
    wx[own_slot, 0:4, :] = w_own[...].astype(jnp.float32)

    @pl.when(even)
    def _():
        for copy in w_even[1:]:
            copy.start()

    @pl.when(odd)
    def _():
        for copy in w_odd:
            copy.start()
        for copy in ahead[1:]:
            copy.start()

    pl.when(even & jnp.logical_not(first))(send_rows)

    def pass_on(k):
        hear(k)
        greet(y_down, flood.at[k + 1])

    pass_on(0)
    pass_on(1)
    to_even.wait_recv()

    @pl.when(odd)
    def _():
        ahead[CHUNKS - 2].wait_send()
        relay.start()

    pass_on(2)
    pass_on(3)

    def tell_behind():
        hear(4)
        greet(behind(-2), flood.at[5])

    @pl.when(even & first)
    def _():
        send_rows()
        tell_behind()

    s_ref[:, :, 0:PAD, :] = jnp.zeros((ROT, 4, PAD, 128), jnp.float32)
    s_ref[:, :, PAD + F :, :] = jnp.zeros((ROT, 4, s_ref.shape[2] - PAD - F, 128), jnp.float32)
    a_ref[0:PAD, :] = jnp.zeros((PAD, 128), jnp.float32)
    a_ref[PAD + F :, :] = jnp.zeros((a_ref.shape[0] - PAD - F, 128), jnp.float32)
    m_ref[...] = jnp.full_like(m_ref, -jnp.inf)

    @pl.when(even)
    def _():
        own_cols.wait()
        weight(0, -2, 0).wait_recv()
        lists.wait_recv()

    @pl.when(odd)
    def _():
        own_rows.wait()
        own_list.wait()
        weight(2, 2, 2).wait_recv()

    weight(1, 1, 1).wait_recv()
    weight(1, 1, 3).wait_recv()
    owners.wait()
    row_weights(wx, a_ref)
    def columns(t, carry):
        column_weights(wx, t + 1, acs_ref.at[t])
        return carry

    lax.fori_loop(0, ROT, columns, 0)

    count = listing.shape[1]
    where, slot_of, start_of = [], [], []
    for n in range(count):
        where.append(owner[listing[3, n]])
        start_of.append(
            (jnp.maximum(listing[0, n] - 1, 0) * 4 + listing[2, n]) * (TALL // 8) + PAD // 8 + listing[1, n] * (PIECE // 8)
        )
        slot = jnp.int32(0)
        for m in range(n):
            slot = slot + jnp.where(where[m] == where[n], 1, 0)
        slot_of.append(slot)
    def planned(k, carry):
        start, there = jnp.int32(0), jnp.int32(0)
        for n in range(count):
            here = where[n] * CAP + slot_of[n] == k
            start = jnp.where(here, start_of[n], start)
            there = jnp.where(here, 1, there)
        plan[0, k] = start
        plan[1, k] = there
        return carry

    lax.fori_loop(0, GROUPS * CAP, planned, 0)

    def half_tile(k, carry):
        h = jnp.where(first, jnp.where(k < 4, k // 2, k - 4), k // 3)
        t = jnp.where(first, jnp.where(k < 4, lax.rem(k, 2), 2), lax.rem(k, 3))

        @pl.when((t == 0) & (h == 0))
        def _():
            to_rows[0].wait_recv()

        @pl.when((t == 0) & (h == 1))
        def _():
            to_rows[1].wait_recv()

        @pl.when((t == 2) & (h == 0))
        def _():
            for c in range(CHUNKS):
                ahead[c].wait_recv()
                passed[c].start()

        pl.when((k == 2) & jnp.logical_not(first))(tell_behind)
        pl.when(k == 4)(functools.partial(hear, 5))
        product(rows, cols, t, s_ref, h * half, half)
        smooth(s_ref, a_ref, acs_ref, t_ref, m_ref, t, h * (F - 8 * HALF_STEP + 12) - 12, HALF_STEP)
        return carry

    def tile(t, carry):
        @pl.when(t == 1)
        def _():
            for c in range(CHUNKS):
                passed[c].wait_recv()

        @pl.when(t == 2)
        def _():
            hear(4)
            relay.wait_recv()

        product(rows, cols, t, s_ref, 0, F)
        smooth(s_ref, a_ref, acs_ref, t_ref, m_ref, t, 0, STEP)
        return carry

    @pl.when(even)
    def _():
        lax.fori_loop(0, 2 * ROT, half_tile, 0)

    @pl.when(odd)
    def _():
        lax.fori_loop(0, ROT, tile, 0)

    def fill(d):
        for s in range(CAP):
            piece = t_ref[pl.ds(plan[0, d * CAP + s] * 8, PIECE), :]
            there = jnp.broadcast_to(plan[1, d * CAP + s], (PIECE, PIECE)) > 0
            piece = jnp.where(there, piece * SCALE, 0.0)
            bucket[d, PIECE * s : PIECE * (s + 1), :] = piece.astype(jnp.bfloat16)

    def piece_copy(d):
        return remote(bucket.at[d], out.at[g], p_send.at[d], p_recv.at[g], (home, d))

    def nth(k):
        j = lax.rem(k + k // 4, 4)
        return peer(lax.rem(j, 2) * 2 + j // 2, 1 - k // 4)

    own_piece = pltpu.make_async_copy(bucket.at[g], out.at[g], loc.at[0])

    def send_pieces(k, carry):
        d = nth(k)
        fill(d)

        @pl.when((k < GROUPS - 1) | even)
        def _():
            piece_copy(d).start()

        @pl.when((k == GROUPS - 1) & odd)
        def _():
            own_piece.start()

        return carry

    pl.when(odd & last)(functools.partial(hear, 7))
    lax.fori_loop(0, GROUPS, send_pieces, 0)

    def best_of(r, carry):
        block = jnp.transpose(m_ref[pl.ds(PAD + 128 * r, 128), :])
        top[pl.ds(r, 1), :] = jnp.max(block, axis=0, keepdims=True) * SCALE
        return carry

    lax.fori_loop(0, 4, best_of, 0)
    top_home = remote(top, best, b_sem.at[0], b_sem.at[1], behind(2))
    top_here = pltpu.make_async_copy(top, best, loc.at[1])

    @pl.when(even)
    def _():
        top_home.start()

    @pl.when(odd)
    def _():
        top_here.start()

    def sent(k, carry):
        piece_copy(nth(k)).wait_send()
        return carry

    lax.fori_loop(0, GROUPS - 1, sent, 0)

    @pl.when(even & last)
    def _():
        greet(behind(1), flood.at[7])

    @pl.when(even)
    def _():
        for copy in w_even:
            copy.wait_send()
        lists.wait_send()
        for copy in to_rows:
            copy.wait_send()
        to_odd.wait_send()
        for copy in passed:
            copy.wait_send()
        top_home.wait()
        piece_copy(g).wait_send()
        piece_copy(g).wait_recv()

    @pl.when(odd)
    def _():
        for copy in w_odd:
            copy.wait_send()
        for k in range(CHUNKS):
            if k != CHUNKS - 2:
                ahead[k].wait_send()
        to_even.wait_send()
        relay.wait_send()
        top_here.wait()
        own_piece.wait()

    def received(k, carry):
        d = nth(k)
        remote(bucket.at[d], out.at[d], p_send.at[d], p_recv.at[d], (home, d)).wait_recv()
        return carry

    lax.fori_loop(0, GROUPS - 1, received, 0)


def settle(out_in, best_in, out, best, sems):
    copies = [
        pltpu.make_async_copy(out_in, out, sems.at[0]),
        pltpu.make_async_copy(best_in, best, sems.at[1]),
    ]
    for copy in copies:
        copy.start()
    for copy in copies:
        copy.wait()


def body(n_blk, embeddings, frame_weight, candidates, owner):
    count = candidates.shape[3]
    dma = pltpu.SemaphoreType.DMA
    hbm, vmem = (pl.BlockSpec(memory_space=m) for m in (pltpu.HBM, pltpu.VMEM))
    out, best = pl.pallas_call(
        functools.partial(kernel, n_blk),
        out_shape=(
            jax.ShapeDtypeStruct((GROUPS, CAP * PIECE, PIECE), jnp.bfloat16),
            jax.ShapeDtypeStruct((4, 128), jnp.float32),
        ),
        in_specs=[hbm] * 4,
        out_specs=(vmem, vmem),
        scratch_shapes=[
            pltpu.SMEM(owner.shape, jnp.int32),
            pltpu.VMEM((4, 128), jnp.bfloat16),
            pltpu.SemaphoreType.REGULAR((8,)),
            pltpu.VMEM((F, D), jnp.bfloat16),
            pltpu.VMEM((ROT, F, D), jnp.bfloat16),
            pltpu.VMEM((4, 8, 128), jnp.float32),
            pltpu.SMEM((4, count), jnp.int32),
            pltpu.SMEM((2, GROUPS * CAP), jnp.int32),
            pltpu.VMEM((ROT, 4, TALL + PAD, 128), jnp.float32),
            pltpu.VMEM((TALL + PAD, 128), jnp.float32),
            pltpu.VMEM((ROT, 2, (STEP + 6 + 7) // 8 * 8, F), jnp.float32),
            pltpu.VMEM((ROT * 4 * TALL, 128), jnp.float32),
            pltpu.VMEM((TALL, 128), jnp.float32),
            pltpu.VMEM((GROUPS, CAP * PIECE, PIECE), jnp.bfloat16),
            pltpu.VMEM((4, 128), jnp.float32),
            dma((4,)),
            dma((1,)),
            dma((3,)),
            dma((2,)),
            dma((2,)),
            dma((CHUNKS,)),
            dma((CHUNKS,)),
            dma((CHUNKS,)),
            dma((CHUNKS,)),
            dma((1,)),
            dma((3,)),
            dma((4,)),
            dma((2,)),
            dma((GROUPS,)),
            dma((GROUPS,)),
            dma((2,)),
        ],
        compiler_params=pltpu.CompilerParams(
            collective_id=0, has_side_effects=True, vmem_limit_bytes=40 << 20
        ),
        name="window_join",
    )(*(
        pltpu.with_memory_space_constraint(x, pltpu.HBM)
        for x in (embeddings, frame_weight.reshape(4, 128), candidates.reshape(4, count), owner)
    ))
    out, best = pl.pallas_call(
        settle,
        out_shape=(
            jax.ShapeDtypeStruct(out.shape, out.dtype),
            jax.ShapeDtypeStruct(best.shape, best.dtype),
        ),
        in_specs=[vmem, vmem],
        out_specs=(hbm, hbm),
        scratch_shapes=[dma((2,))],
        name="settle",
    )(*(pltpu.with_memory_space_constraint(x, pltpu.VMEM) for x in (out, best)))
    return best.reshape(F), out.reshape(1, 1, GROUPS, CAP, PIECE, PIECE)


def solution(mesh):
    return jax.shard_map(
        functools.partial(body, mesh.shape["blk"]),
        mesh=mesh,
        in_specs=(P(("blk", "grp"), None), P(("blk", "grp")), P("blk", "grp", None, None), P()),
        out_specs=(P(("blk", "grp")), P("blk", "grp", None, None, None, None)),
        check_vma=False,
    )
```

```python
import functools

import jax
import jax.numpy as jnp
from jax import lax
from jax.experimental import pallas as pl
from jax.experimental.pallas import tpu as pltpu
from jax.sharding import PartitionSpec as P

MESH = pl.DeviceIdType.MESH
F = 512
D = 512
PIECE = 128
CAP = 2
ROT = 3
GROUPS = 8
STEP = 65
HALF_STEP = 33
PAD = 16
TALL = PAD + 8 * STEP
CHUNKS = 4
SCALE = D ** (-0.5)


def rotate_left(x, n):
    n %= F
    return x if n == 0 else pltpu.roll(x, F - n, 1)


def four(x):
    return jnp.concatenate([x] * 4, axis=1)


def column_weights(w_ref, slot, acs_ref):
    lane = lax.broadcasted_iota(jnp.int32, (8, 128), 1)
    sub = lax.broadcasted_iota(jnp.int32, (8, F), 0)
    rows = [jnp.broadcast_to(w_ref[slot, c : c + 1, :], (8, 128)) for c in range(4)]
    for k in range(2):
        kept = list(rows)
        if k == 0:
            kept[0] = jnp.where(lane == 0, 0.0, kept[0])
        else:
            kept[3] = jnp.where(lane == 127, 0.0, kept[3])
        x = jnp.concatenate(kept, axis=1)
        for bit in (1, 2, 4):
            x = jnp.where((sub & bit) != 0, rotate_left(x, bit), x)
        for m in range((STEP + 6 + 7) // 8):
            acs_ref[k, 8 * m : 8 * m + 8, :] = rotate_left(x, 8 * m - 3)


def row_weights(w_ref, a_ref):
    for r in range(4):
        wide = jnp.broadcast_to(w_ref[0, r : r + 1, :], (128, 128))
        a_ref[PAD + 128 * r : PAD + 128 * (r + 1), :] = jnp.transpose(wide) * 0.25


def product(r_ref, c_ref, t, s_ref, row, count):
    for h in range(2):
        part = lax.dot_general(
            r_ref[pl.ds(row, count), :],
            c_ref[t, 256 * h : 256 * (h + 1), :],
            (((1,), (1,)), ((), ())),
            preferred_element_type=jnp.float32,
        )
        for k in range(2):
            s_ref[t, 2 * h + k, pl.ds(PAD + row, count), :] = part[:, 128 * k : 128 * (k + 1)]


def smooth(s_ref, a_ref, acs_ref, t_ref, m_ref, t, row, step):
    levels, weights = {}, {}

    def level(n, q):
        if (n, q) not in levels:
            if n == 0:
                rows = [s_ref[t, c, pl.ds(PAD + row + q, 8, stride=step), :] for c in range(4)]
                levels[n, q] = rotate_left(jnp.concatenate(rows, axis=1), q)
            else:
                if q not in weights:
                    a = four(a_ref[pl.ds(PAD + row + q, 8, stride=step), :])
                    weights[q] = (
                        a * acs_ref[t, 0, q + 3 : q + 4, :],
                        a * acs_ref[t, 1, q + 3 : q + 4, :],
                    )
                before, after = weights[q]
                levels[n, q] = (
                    level(n - 1, q) + before * level(n - 1, q - 1) + after * level(n - 1, q + 1)
                )
        return levels[n, q]

    for q in range(step):
        x = level(3, q)
        widest = jnp.maximum(
            jnp.maximum(x[:, :128], x[:, 128:256]), jnp.maximum(x[:, 256:384], x[:, 384:])
        )
        where = pl.ds(PAD + row + q, 8, stride=step)
        m_ref[where, :] = jnp.maximum(m_ref[where, :], widest)
        x = rotate_left(x, -q)
        for c in range(4):
            where = pl.ds((t * 4 + c) * TALL + PAD + row + q, 8, stride=step)
            t_ref[where, :] = x[:, 128 * c : 128 * (c + 1)]


def kernel(
    n_blk,
    emb,
    w_in,
    cand,
    owner_in,
    out,
    best,
    owner,
    w_own,
    flood,
    rows,
    cols,
    wx,
    listing,
    plan,
    s_ref,
    a_ref,
    acs_ref,
    t_ref,
    m_ref,
    bucket,
    top,
    loc,
    e_send,
    e_recv,
    r_send,
    r_recv,
    z_send,
    z_recv,
    f_send,
    f_recv,
    y_send,
    y_recv,
    w_send,
    w_recv,
    c_sem,
    p_send,
    p_recv,
    b_sem,
):
    b, g = lax.axis_index("blk"), lax.axis_index("grp")
    core = lax.rem(b, 2)
    even, odd = core == 0, core == 1
    home = lax.rem(b + 2 * (1 - core), n_blk)

    def behind(k):
        return (lax.rem(b + k + n_blk, n_blk), g)

    def peer(dx, dy):
        return lax.rem(g // 2 + dx, 4) * 2 + lax.rem(g + dy, 2)

    def remote(src, dst, send, recv, device):
        return pltpu.make_async_remote_copy(
            src_ref=src, dst_ref=dst, send_sem=send, recv_sem=recv, device_id=device, device_id_type=MESH
        )

    barrier = pltpu.get_barrier_semaphore()
    order = [(0, 1), (2, 1), (1, 1), (3, 1), (2, 0), (1, 0), (3, 0)]
    per_row = n_blk // 4
    turn = 1 - 2 * lax.rem(g, 2)
    y_lo = b // per_row
    y_down = (lax.rem(b - per_row + n_blk, n_blk), g + jnp.where(y_lo == 0, turn, 0))
    y_up = (lax.rem(b + per_row, n_blk), g + jnp.where(y_lo == 3, turn, 0))

    def greet(device, semaphore=barrier):
        pl.semaphore_signal(semaphore, inc=1, device_id=device, device_id_type=MESH)

    @pl.when(even)
    def _():
        greet(behind(-2))
        greet(behind(1))
        greet(behind(-1))

    @pl.when(odd)
    def _():
        greet(behind(-1))
        greet(behind(-2))
        greet(behind(-3))

    greet((b, peer(1, 0)))
    greet((b, peer(3, 0)))
    greet(y_up)

    own_rows = pltpu.make_async_copy(emb, rows, loc.at[0])
    own_cols = pltpu.make_async_copy(emb, cols.at[1], loc.at[0])
    own_list = pltpu.make_async_copy(cand, listing, loc.at[1])
    own_weights = pltpu.make_async_copy(w_in, w_own, loc.at[2])
    owners = pltpu.make_async_copy(owner_in, owner, loc.at[3])
    own_weights.start()

    @pl.when(even)
    def _():
        own_cols.start()

    @pl.when(odd)
    def _():
        own_rows.start()
        own_list.start()

    owners.start()
    own_slot = 2 * (1 - core)
    own_weights.wait()
    wx[own_slot, 0:4, :] = w_own[...].astype(jnp.float32)
    pl.semaphore_wait(barrier, 6)

    quarter = F // CHUNKS
    to_odd = remote(emb, cols.at[0], e_send.at[0], e_recv.at[1], behind(1))
    half = F // 2
    to_rows = [
        remote(
            emb.at[pl.ds(k * half, half)], rows.at[pl.ds(k * half, half)], r_send.at[k], r_recv.at[k], behind(-2)
        )
        for k in range(2)
    ]
    to_even = remote(emb, cols.at[0], e_send.at[0], e_recv.at[1], behind(-1))

    def chunk(ref, k):
        return ref.at[pl.ds(k * quarter, quarter)]

    ahead = [
        remote(chunk(emb, k), chunk(cols.at[2], k), z_send.at[k], z_recv.at[k], behind(1))
        for k in range(CHUNKS)
    ]
    passed = [
        remote(chunk(cols.at[2], k), chunk(cols.at[1], k), f_send.at[k], f_recv.at[k], behind(1))
        for k in range(CHUNKS)
    ]
    relay = [
        remote(chunk(cols.at[0], k), chunk(cols.at[2], k), y_send.at[k], y_recv.at[k], behind(2))
        for k in range(CHUNKS)
    ]

    def weight(k, steps, slot):
        return remote(wx.at[own_slot], wx.at[slot], w_send.at[k], w_recv.at[slot], behind(steps))

    w_even = [weight(0, -2, 0), weight(1, 1, 1), weight(2, 3, 3)]
    w_odd = [weight(0, -1, 1), weight(1, 1, 3), weight(2, 2, 2)]
    lists = remote(cand, listing, c_sem.at[0], c_sem.at[1], behind(-2))

    first = lax.rem(b // 2, 8) == 0
    last = lax.rem(b // 2, 8) == 7

    def send_rows():
        hear(6)
        w_even[0].start()
        lists.start()
        for copy in to_rows:
            copy.start()

    def hear(k):
        pl.semaphore_wait(flood.at[k], 1)

    @pl.when(even)
    def _():
        greet(behind(2), flood.at[6])
        for copy in w_even[1:]:
            copy.start()
        to_odd.start()

    @pl.when(odd)
    def _():
        for copy in w_odd:
            copy.start()
        to_even.start()
        for copy in ahead:
            copy.start()

    greet((b, peer(3, 0)), flood.at[0])
    pl.when(even & jnp.logical_not(first))(send_rows)
    for k in range(4):
        hear(k)
        greet(y_down, flood.at[k + 1])

    def tell_behind():
        hear(4)
        greet(behind(-2), flood.at[5])

    @pl.when(even & first)
    def _():
        send_rows()
        tell_behind()

    to_even.wait_recv()

    @pl.when(odd)
    def _():
        ahead[CHUNKS - 2].wait_send()
        for copy in relay:
            copy.start()

    s_ref[:, :, 0:PAD, :] = jnp.zeros((ROT, 4, PAD, 128), jnp.float32)
    s_ref[:, :, PAD + F :, :] = jnp.zeros((ROT, 4, s_ref.shape[2] - PAD - F, 128), jnp.float32)
    a_ref[0:PAD, :] = jnp.zeros((PAD, 128), jnp.float32)
    a_ref[PAD + F :, :] = jnp.zeros((a_ref.shape[0] - PAD - F, 128), jnp.float32)
    m_ref[...] = jnp.full_like(m_ref, -jnp.inf)

    @pl.when(even)
    def _():
        own_cols.wait()
        weight(0, -2, 0).wait_recv()
        lists.wait_recv()

    @pl.when(odd)
    def _():
        own_rows.wait()
        own_list.wait()
        weight(2, 2, 2).wait_recv()

    weight(1, 1, 1).wait_recv()
    weight(1, 1, 3).wait_recv()
    owners.wait()
    row_weights(wx, a_ref)
    for t in range(ROT):
        column_weights(wx, t + 1, acs_ref.at[t])

    count = listing.shape[1]
    where, slot_of, start_of = [], [], []
    for n in range(count):
        where.append(owner[listing[3, n]])
        start_of.append(
            (jnp.maximum(listing[0, n] - 1, 0) * 4 + listing[2, n]) * (TALL // 8) + PAD // 8 + listing[1, n] * (PIECE // 8)
        )
        slot = jnp.int32(0)
        for m in range(n):
            slot = slot + jnp.where(where[m] == where[n], 1, 0)
        slot_of.append(slot)
    for d in range(GROUPS):
        for s in range(CAP):
            start, there = jnp.int32(0), jnp.int32(0)
            for n in range(count):
                here = (where[n] == d) & (slot_of[n] == s)
                start = jnp.where(here, start_of[n], start)
                there = jnp.where(here, 1, there)
            plan[0, d * CAP + s] = start
            plan[1, d * CAP + s] = there

    def half_tile(k, carry):
        h = jnp.where(first, jnp.where(k < 4, k // 2, k - 4), k // 3)
        t = jnp.where(first, jnp.where(k < 4, lax.rem(k, 2), 2), lax.rem(k, 3))

        @pl.when((t == 0) & (h == 0))
        def _():
            to_rows[0].wait_recv()

        @pl.when((t == 0) & (h == 1))
        def _():
            to_rows[1].wait_recv()

        @pl.when((t == 2) & (h == 0))
        def _():
            for c in range(CHUNKS):
                ahead[c].wait_recv()
                passed[c].start()

        pl.when((k == 2) & jnp.logical_not(first))(tell_behind)
        pl.when(k == 4)(functools.partial(hear, 5))
        product(rows, cols, t, s_ref, h * half, half)
        smooth(s_ref, a_ref, acs_ref, t_ref, m_ref, t, h * (F - 8 * HALF_STEP + 12) - 12, HALF_STEP)
        return carry

    def tile(t, carry):
        @pl.when(t == 1)
        def _():
            for c in range(CHUNKS):
                passed[c].wait_recv()

        @pl.when(t == 2)
        def _():
            hear(4)
            for copy in relay:
                copy.wait_recv()

        product(rows, cols, t, s_ref, 0, F)
        smooth(s_ref, a_ref, acs_ref, t_ref, m_ref, t, 0, STEP)
        return carry

    @pl.when(even)
    def _():
        lax.fori_loop(0, 2 * ROT, half_tile, 0)

    @pl.when(odd)
    def _():
        lax.fori_loop(0, ROT, tile, 0)

    def fill(d):
        for s in range(CAP):
            piece = t_ref[pl.ds(plan[0, d * CAP + s] * 8, PIECE), :]
            there = jnp.broadcast_to(plan[1, d * CAP + s], (PIECE, PIECE)) > 0
            piece = jnp.where(there, piece * SCALE, 0.0)
            bucket[d, PIECE * s : PIECE * (s + 1), :] = piece.astype(jnp.bfloat16)

    def piece_copy(d):
        return remote(bucket.at[d], out.at[g], p_send.at[d], p_recv.at[g], (home, d))

    pl.when(odd & last)(functools.partial(hear, 7))
    for dx, dy in order:
        d = peer(dx, dy)
        fill(d)
        piece_copy(d).start()
    fill(g)
    own_piece = pltpu.make_async_copy(bucket.at[g], out.at[g], loc.at[0])

    @pl.when(even)
    def _():
        piece_copy(g).start()

    @pl.when(odd)
    def _():
        own_piece.start()

    for r in range(4):
        block = jnp.transpose(m_ref[PAD + 128 * r : PAD + 128 * (r + 1), :])
        top[r : r + 1, :] = jnp.max(block, axis=0, keepdims=True) * SCALE
    top_home = remote(top, best, b_sem.at[0], b_sem.at[1], behind(2))
    top_here = pltpu.make_async_copy(top, best, loc.at[1])

    @pl.when(even)
    def _():
        top_home.start()

    @pl.when(odd)
    def _():
        top_here.start()

    for dx, dy in order:
        piece_copy(peer(dx, dy)).wait_send()

    @pl.when(even & last)
    def _():
        greet(behind(1), flood.at[7])

    @pl.when(even)
    def _():
        for copy in w_even:
            copy.wait_send()
        lists.wait_send()
        for copy in to_rows:
            copy.wait_send()
        to_odd.wait_send()
        for copy in passed:
            copy.wait_send()
        top_home.wait()
        piece_copy(g).wait_send()
        piece_copy(g).wait_recv()

    @pl.when(odd)
    def _():
        for copy in w_odd:
            copy.wait_send()
        for k in range(CHUNKS):
            if k != CHUNKS - 2:
                ahead[k].wait_send()
        to_even.wait_send()
        for copy in relay:
            copy.wait_send()
        top_here.wait()
        own_piece.wait()

    for dx, dy in order:
        d = peer(dx, dy)
        remote(bucket.at[d], out.at[d], p_send.at[d], p_recv.at[d], (home, d)).wait_recv()


def settle(out_in, best_in, out, best, sems):
    copies = [
        pltpu.make_async_copy(out_in, out, sems.at[0]),
        pltpu.make_async_copy(best_in, best, sems.at[1]),
    ]
    for copy in copies:
        copy.start()
    for copy in copies:
        copy.wait()


def body(n_blk, embeddings, frame_weight, candidates, owner):
    count = candidates.shape[3]
    dma = pltpu.SemaphoreType.DMA
    hbm, vmem = (pl.BlockSpec(memory_space=m) for m in (pltpu.HBM, pltpu.VMEM))
    out, best = pl.pallas_call(
        functools.partial(kernel, n_blk),
        out_shape=(
            jax.ShapeDtypeStruct((GROUPS, CAP * PIECE, PIECE), jnp.bfloat16),
            jax.ShapeDtypeStruct((4, 128), jnp.float32),
        ),
        in_specs=[hbm] * 4,
        out_specs=(vmem, vmem),
        scratch_shapes=[
            pltpu.SMEM(owner.shape, jnp.int32),
            pltpu.VMEM((4, 128), jnp.bfloat16),
            pltpu.SemaphoreType.REGULAR((8,)),
            pltpu.VMEM((F, D), jnp.bfloat16),
            pltpu.VMEM((ROT, F, D), jnp.bfloat16),
            pltpu.VMEM((4, 8, 128), jnp.float32),
            pltpu.SMEM((4, count), jnp.int32),
            pltpu.SMEM((2, GROUPS * CAP), jnp.int32),
            pltpu.VMEM((ROT, 4, TALL + PAD, 128), jnp.float32),
            pltpu.VMEM((TALL + PAD, 128), jnp.float32),
            pltpu.VMEM((ROT, 2, (STEP + 6 + 7) // 8 * 8, F), jnp.float32),
            pltpu.VMEM((ROT * 4 * TALL, 128), jnp.float32),
            pltpu.VMEM((TALL, 128), jnp.float32),
            pltpu.VMEM((GROUPS, CAP * PIECE, PIECE), jnp.bfloat16),
            pltpu.VMEM((4, 128), jnp.float32),
            dma((4,)),
            dma((1,)),
            dma((3,)),
            dma((2,)),
            dma((2,)),
            dma((CHUNKS,)),
            dma((CHUNKS,)),
            dma((CHUNKS,)),
            dma((CHUNKS,)),
            dma((CHUNKS,)),
            dma((CHUNKS,)),
            dma((3,)),
            dma((4,)),
            dma((2,)),
            dma((GROUPS,)),
            dma((GROUPS,)),
            dma((2,)),
        ],
        compiler_params=pltpu.CompilerParams(
            collective_id=0, has_side_effects=True, vmem_limit_bytes=40 << 20
        ),
        name="window_join",
    )(*(
        pltpu.with_memory_space_constraint(x, pltpu.HBM)
        for x in (embeddings, frame_weight.reshape(4, 128), candidates.reshape(4, count), owner)
    ))
    out, best = pl.pallas_call(
        settle,
        out_shape=(
            jax.ShapeDtypeStruct(out.shape, out.dtype),
            jax.ShapeDtypeStruct(best.shape, best.dtype),
        ),
        in_specs=[vmem, vmem],
        out_specs=(hbm, hbm),
        scratch_shapes=[dma((2,))],
        name="settle",
    )(*(pltpu.with_memory_space_constraint(x, pltpu.VMEM) for x in (out, best)))
    return best.reshape(F), out.reshape(1, 1, GROUPS, CAP, PIECE, PIECE)


def solution(mesh):
    return jax.shard_map(
        functools.partial(body, mesh.shape["blk"]),
        mesh=mesh,
        in_specs=(P(("blk", "grp"), None), P(("blk", "grp")), P("blk", "grp", None, None), P()),
        out_specs=(P(("blk", "grp")), P("blk", "grp", None, None, None, None)),
        check_vma=False,
    )
```

```python
import functools

import jax
import jax.numpy as jnp
from jax import lax
from jax.experimental import pallas as pl
from jax.experimental.pallas import tpu as pltpu
from jax.sharding import PartitionSpec as P

MESH = pl.DeviceIdType.MESH
F = 512
D = 512
PIECE = 128
CAP = 2
ROT = 3
GROUPS = 8
STEP = 65
HALF_STEP = 33
PAD = 16
TALL = PAD + 8 * STEP
CHUNKS = 4
SCALE = D ** (-0.5)


def rotate_left(x, n):
    n %= F
    return x if n == 0 else pltpu.roll(x, F - n, 1)


def four(x):
    return jnp.concatenate([x] * 4, axis=1)


def column_weights(w_ref, slot, acs_ref):
    lane = lax.broadcasted_iota(jnp.int32, (8, 128), 1)
    sub = lax.broadcasted_iota(jnp.int32, (8, F), 0)
    rows = [jnp.broadcast_to(w_ref[slot, c : c + 1, :], (8, 128)) for c in range(4)]
    for k in range(2):
        kept = list(rows)
        if k == 0:
            kept[0] = jnp.where(lane == 0, 0.0, kept[0])
        else:
            kept[3] = jnp.where(lane == 127, 0.0, kept[3])
        x = jnp.concatenate(kept, axis=1)
        for bit in (1, 2, 4):
            x = jnp.where((sub & bit) != 0, rotate_left(x, bit), x)
        for m in range((STEP + 6 + 7) // 8):
            acs_ref[k, 8 * m : 8 * m + 8, :] = rotate_left(x, 8 * m - 3)


def row_weights(w_ref, a_ref):
    for r in range(4):
        wide = jnp.broadcast_to(w_ref[0, r : r + 1, :], (128, 128))
        a_ref[PAD + 128 * r : PAD + 128 * (r + 1), :] = jnp.transpose(wide) * 0.25


def product(r_ref, c_ref, t, s_ref, row, count):
    for h in range(2):
        part = lax.dot_general(
            r_ref[pl.ds(row, count), :],
            c_ref[t, 256 * h : 256 * (h + 1), :],
            (((1,), (1,)), ((), ())),
            preferred_element_type=jnp.float32,
        )
        for k in range(2):
            s_ref[t, 2 * h + k, pl.ds(PAD + row, count), :] = part[:, 128 * k : 128 * (k + 1)]


def smooth(s_ref, a_ref, acs_ref, t_ref, m_ref, t, row, step):
    levels, weights = {}, {}

    def level(n, q):
        if (n, q) not in levels:
            if n == 0:
                rows = [s_ref[t, c, pl.ds(PAD + row + q, 8, stride=step), :] for c in range(4)]
                levels[n, q] = rotate_left(jnp.concatenate(rows, axis=1), q)
            else:
                if q not in weights:
                    a = four(a_ref[pl.ds(PAD + row + q, 8, stride=step), :])
                    weights[q] = (
                        a * acs_ref[t, 0, q + 3 : q + 4, :],
                        a * acs_ref[t, 1, q + 3 : q + 4, :],
                    )
                before, after = weights[q]
                levels[n, q] = (
                    level(n - 1, q) + before * level(n - 1, q - 1) + after * level(n - 1, q + 1)
                )
        return levels[n, q]

    for q in range(step):
        x = level(3, q)
        widest = jnp.maximum(
            jnp.maximum(x[:, :128], x[:, 128:256]), jnp.maximum(x[:, 256:384], x[:, 384:])
        )
        where = pl.ds(PAD + row + q, 8, stride=step)
        m_ref[where, :] = jnp.maximum(m_ref[where, :], widest)
        x = rotate_left(x, -q)
        for c in range(4):
            where = pl.ds((t * 4 + c) * TALL + PAD + row + q, 8, stride=step)
            t_ref[where, :] = x[:, 128 * c : 128 * (c + 1)]


def kernel(
    n_blk,
    emb,
    w_in,
    cand,
    owner_in,
    out,
    best,
    owner,
    w_own,
    flood,
    rows,
    cols,
    wx,
    listing,
    plan,
    s_ref,
    a_ref,
    acs_ref,
    t_ref,
    m_ref,
    bucket,
    top,
    loc,
    e_send,
    e_recv,
    r_send,
    r_recv,
    z_send,
    z_recv,
    f_send,
    f_recv,
    y_send,
    y_recv,
    w_send,
    w_recv,
    c_sem,
    p_send,
    p_recv,
    b_sem,
):
    b, g = lax.axis_index("blk"), lax.axis_index("grp")
    core = lax.rem(b, 2)
    even, odd = core == 0, core == 1
    home = lax.rem(b + 2 * (1 - core), n_blk)

    def behind(k):
        return (lax.rem(b + k + n_blk, n_blk), g)

    def peer(dx, dy):
        return lax.rem(g // 2 + dx, 4) * 2 + lax.rem(g + dy, 2)

    def remote(src, dst, send, recv, device):
        return pltpu.make_async_remote_copy(
            src_ref=src, dst_ref=dst, send_sem=send, recv_sem=recv, device_id=device, device_id_type=MESH
        )

    barrier = pltpu.get_barrier_semaphore()
    order = [(0, 1), (2, 1), (1, 1), (3, 1), (2, 0), (1, 0), (3, 0)]
    per_row = n_blk // 4
    turn = 1 - 2 * lax.rem(g, 2)
    y_lo = b // per_row
    y_down = (lax.rem(b - per_row + n_blk, n_blk), g + jnp.where(y_lo == 0, turn, 0))
    y_up = (lax.rem(b + per_row, n_blk), g + jnp.where(y_lo == 3, turn, 0))

    def greet(device, semaphore=barrier):
        pl.semaphore_signal(semaphore, inc=1, device_id=device, device_id_type=MESH)

    @pl.when(even)
    def _():
        greet(behind(-2))
        greet(behind(1))
        greet(behind(-1))

    @pl.when(odd)
    def _():
        greet(behind(-1))
        greet(behind(-2))
        greet(behind(-3))

    greet((b, peer(1, 0)))
    greet((b, peer(3, 0)))
    greet(y_up)

    own_rows = pltpu.make_async_copy(emb, rows, loc.at[0])
    own_cols = pltpu.make_async_copy(emb, cols.at[1], loc.at[0])
    own_list = pltpu.make_async_copy(cand, listing, loc.at[1])
    own_weights = pltpu.make_async_copy(w_in, w_own, loc.at[2])
    owners = pltpu.make_async_copy(owner_in, owner, loc.at[3])
    own_weights.start()

    @pl.when(even)
    def _():
        own_cols.start()

    @pl.when(odd)
    def _():
        own_rows.start()
        own_list.start()

    owners.start()
    own_slot = 2 * (1 - core)
    own_weights.wait()
    wx[own_slot, 0:4, :] = w_own[...].astype(jnp.float32)
    pl.semaphore_wait(barrier, 6)

    quarter = F // CHUNKS
    to_odd = remote(emb, cols.at[0], e_send.at[0], e_recv.at[1], behind(1))
    half = F // 2
    to_rows = [
        remote(
            emb.at[pl.ds(k * half, half)], rows.at[pl.ds(k * half, half)], r_send.at[k], r_recv.at[k], behind(-2)
        )
        for k in range(2)
    ]
    to_even = remote(emb, cols.at[0], e_send.at[0], e_recv.at[1], behind(-1))

    def chunk(ref, k):
        return ref.at[pl.ds(k * quarter, quarter)]

    ahead = [
        remote(chunk(emb, k), chunk(cols.at[2], k), z_send.at[k], z_recv.at[k], behind(1))
        for k in range(CHUNKS)
    ]
    passed = [
        remote(chunk(cols.at[2], k), chunk(cols.at[1], k), f_send.at[k], f_recv.at[k], behind(1))
        for k in range(CHUNKS)
    ]
    relay = [
        remote(chunk(cols.at[0], k), chunk(cols.at[2], k), y_send.at[k], y_recv.at[k], behind(2))
        for k in range(CHUNKS)
    ]

    def weight(k, steps, slot):
        return remote(wx.at[own_slot], wx.at[slot], w_send.at[k], w_recv.at[slot], behind(steps))

    w_even = [weight(0, -2, 0), weight(1, 1, 1), weight(2, 3, 3)]
    w_odd = [weight(0, -1, 1), weight(1, 1, 3), weight(2, 2, 2)]
    lists = remote(cand, listing, c_sem.at[0], c_sem.at[1], behind(-2))

    first = lax.rem(b // 2, 8) == 0
    last = lax.rem(b // 2, 8) == 7

    def send_rows():
        hear(6)
        w_even[0].start()
        lists.start()
        for copy in to_rows:
            copy.start()

    def hear(k):
        pl.semaphore_wait(flood.at[k], 1)

    @pl.when(even)
    def _():
        greet(behind(2), flood.at[6])
        for copy in w_even[1:]:
            copy.start()
        to_odd.start()

    @pl.when(odd)
    def _():
        for copy in w_odd:
            copy.start()
        to_even.start()
        for copy in ahead:
            copy.start()

    greet((b, peer(3, 0)), flood.at[0])
    pl.when(even & jnp.logical_not(first))(send_rows)
    for k in range(4):
        hear(k)
        greet(y_down, flood.at[k + 1])

    def tell_behind():
        hear(4)
        greet(behind(-2), flood.at[5])

    @pl.when(even & first)
    def _():
        send_rows()
        tell_behind()

    to_even.wait_recv()

    @pl.when(odd)
    def _():
        ahead[CHUNKS - 2].wait_send()
        for copy in relay:
            copy.start()

    s_ref[:, :, 0:PAD, :] = jnp.zeros((ROT, 4, PAD, 128), jnp.float32)
    s_ref[:, :, PAD + F :, :] = jnp.zeros((ROT, 4, s_ref.shape[2] - PAD - F, 128), jnp.float32)
    a_ref[0:PAD, :] = jnp.zeros((PAD, 128), jnp.float32)
    a_ref[PAD + F :, :] = jnp.zeros((a_ref.shape[0] - PAD - F, 128), jnp.float32)
    m_ref[...] = jnp.full_like(m_ref, -jnp.inf)

    @pl.when(even)
    def _():
        own_cols.wait()
        weight(0, -2, 0).wait_recv()
        lists.wait_recv()

    @pl.when(odd)
    def _():
        own_rows.wait()
        own_list.wait()
        weight(2, 2, 2).wait_recv()

    weight(1, 1, 1).wait_recv()
    weight(1, 1, 3).wait_recv()
    owners.wait()
    row_weights(wx, a_ref)
    for t in range(ROT):
        column_weights(wx, t + 1, acs_ref.at[t])

    count = listing.shape[1]
    where, slot_of, start_of = [], [], []
    for n in range(count):
        where.append(owner[listing[3, n]])
        start_of.append(
            (jnp.maximum(listing[0, n] - 1, 0) * 4 + listing[2, n]) * (TALL // 8) + PAD // 8 + listing[1, n] * (PIECE // 8)
        )
        slot = jnp.int32(0)
        for m in range(n):
            slot = slot + jnp.where(where[m] == where[n], 1, 0)
        slot_of.append(slot)
    for d in range(GROUPS):
        for s in range(CAP):
            start, there = jnp.int32(0), jnp.int32(0)
            for n in range(count):
                here = (where[n] == d) & (slot_of[n] == s)
                start = jnp.where(here, start_of[n], start)
                there = jnp.where(here, 1, there)
            plan[0, d * CAP + s] = start
            plan[1, d * CAP + s] = there

    def half_tile(k, carry):
        h = k // 3
        t = lax.rem(k, 3)

        @pl.when((t == 0) & (h == 0))
        def _():
            to_rows[0].wait_recv()

        @pl.when((t == 0) & (h == 1))
        def _():
            to_rows[1].wait_recv()

        @pl.when((t == 2) & (h == 0))
        def _():
            for c in range(CHUNKS):
                ahead[c].wait_recv()
                passed[c].start()

        pl.when(k == 2)(tell_behind)
        pl.when(k == 4)(functools.partial(hear, 5))
        product(rows, cols, t, s_ref, h * half, half)
        smooth(s_ref, a_ref, acs_ref, t_ref, m_ref, t, h * (F - 8 * HALF_STEP + 12) - 12, HALF_STEP)
        return carry

    def tile(t, carry):
        @pl.when(even & (t == 0))
        def _():
            for copy in to_rows:
                copy.wait_recv()

        @pl.when(even & (t == 2))
        def _():
            hear(5)
            for c in range(CHUNKS):
                ahead[c].wait_recv()
                passed[c].start()

        @pl.when(odd & (t == 1))
        def _():
            for c in range(CHUNKS):
                passed[c].wait_recv()

        @pl.when(odd & (t == 2))
        def _():
            hear(4)
            for copy in relay:
                copy.wait_recv()

        product(rows, cols, t, s_ref, 0, F)
        smooth(s_ref, a_ref, acs_ref, t_ref, m_ref, t, 0, STEP)
        return carry

    @pl.when(even & jnp.logical_not(first))
    def _():
        lax.fori_loop(0, 2 * ROT, half_tile, 0)

    @pl.when(odd | first)
    def _():
        lax.fori_loop(0, ROT, tile, 0)

    def fill(d):
        for s in range(CAP):
            piece = t_ref[pl.ds(plan[0, d * CAP + s] * 8, PIECE), :]
            there = jnp.broadcast_to(plan[1, d * CAP + s], (PIECE, PIECE)) > 0
            piece = jnp.where(there, piece * SCALE, 0.0)
            bucket[d, PIECE * s : PIECE * (s + 1), :] = piece.astype(jnp.bfloat16)

    def piece_copy(d):
        return remote(bucket.at[d], out.at[g], p_send.at[d], p_recv.at[g], (home, d))

    pl.when(odd & last)(functools.partial(hear, 7))
    for dx, dy in order:
        d = peer(dx, dy)
        fill(d)
        piece_copy(d).start()
    fill(g)
    own_piece = pltpu.make_async_copy(bucket.at[g], out.at[g], loc.at[0])

    @pl.when(even)
    def _():
        piece_copy(g).start()

    @pl.when(odd)
    def _():
        own_piece.start()

    for r in range(4):
        block = jnp.transpose(m_ref[PAD + 128 * r : PAD + 128 * (r + 1), :])
        top[r : r + 1, :] = jnp.max(block, axis=0, keepdims=True) * SCALE
    top_home = remote(top, best, b_sem.at[0], b_sem.at[1], behind(2))
    top_here = pltpu.make_async_copy(top, best, loc.at[1])

    @pl.when(even)
    def _():
        top_home.start()

    @pl.when(odd)
    def _():
        top_here.start()

    for dx, dy in order:
        piece_copy(peer(dx, dy)).wait_send()

    @pl.when(even & last)
    def _():
        greet(behind(1), flood.at[7])

    @pl.when(even)
    def _():
        for copy in w_even:
            copy.wait_send()
        lists.wait_send()
        for copy in to_rows:
            copy.wait_send()
        to_odd.wait_send()
        for copy in passed:
            copy.wait_send()
        top_home.wait()
        piece_copy(g).wait_send()
        piece_copy(g).wait_recv()

    @pl.when(odd)
    def _():
        for copy in w_odd:
            copy.wait_send()
        for k in range(CHUNKS):
            if k != CHUNKS - 2:
                ahead[k].wait_send()
        to_even.wait_send()
        for copy in relay:
            copy.wait_send()
        top_here.wait()
        own_piece.wait()

    for dx, dy in order:
        d = peer(dx, dy)
        remote(bucket.at[d], out.at[d], p_send.at[d], p_recv.at[d], (home, d)).wait_recv()


def settle(out_in, best_in, out, best, sems):
    copies = [
        pltpu.make_async_copy(out_in, out, sems.at[0]),
        pltpu.make_async_copy(best_in, best, sems.at[1]),
    ]
    for copy in copies:
        copy.start()
    for copy in copies:
        copy.wait()


def body(n_blk, embeddings, frame_weight, candidates, owner):
    count = candidates.shape[3]
    dma = pltpu.SemaphoreType.DMA
    hbm, vmem = (pl.BlockSpec(memory_space=m) for m in (pltpu.HBM, pltpu.VMEM))
    out, best = pl.pallas_call(
        functools.partial(kernel, n_blk),
        out_shape=(
            jax.ShapeDtypeStruct((GROUPS, CAP * PIECE, PIECE), jnp.bfloat16),
            jax.ShapeDtypeStruct((4, 128), jnp.float32),
        ),
        in_specs=[hbm] * 4,
        out_specs=(vmem, vmem),
        scratch_shapes=[
            pltpu.SMEM(owner.shape, jnp.int32),
            pltpu.VMEM((4, 128), jnp.bfloat16),
            pltpu.SemaphoreType.REGULAR((8,)),
            pltpu.VMEM((F, D), jnp.bfloat16),
            pltpu.VMEM((ROT, F, D), jnp.bfloat16),
            pltpu.VMEM((4, 8, 128), jnp.float32),
            pltpu.SMEM((4, count), jnp.int32),
            pltpu.SMEM((2, GROUPS * CAP), jnp.int32),
            pltpu.VMEM((ROT, 4, TALL + PAD, 128), jnp.float32),
            pltpu.VMEM((TALL + PAD, 128), jnp.float32),
            pltpu.VMEM((ROT, 2, (STEP + 6 + 7) // 8 * 8, F), jnp.float32),
            pltpu.VMEM((ROT * 4 * TALL, 128), jnp.float32),
            pltpu.VMEM((TALL, 128), jnp.float32),
            pltpu.VMEM((GROUPS, CAP * PIECE, PIECE), jnp.bfloat16),
            pltpu.VMEM((4, 128), jnp.float32),
            dma((4,)),
            dma((1,)),
            dma((3,)),
            dma((2,)),
            dma((2,)),
            dma((CHUNKS,)),
            dma((CHUNKS,)),
            dma((CHUNKS,)),
            dma((CHUNKS,)),
            dma((CHUNKS,)),
            dma((CHUNKS,)),
            dma((3,)),
            dma((4,)),
            dma((2,)),
            dma((GROUPS,)),
            dma((GROUPS,)),
            dma((2,)),
        ],
        compiler_params=pltpu.CompilerParams(
            collective_id=0, has_side_effects=True, vmem_limit_bytes=40 << 20
        ),
        name="window_join",
    )(*(
        pltpu.with_memory_space_constraint(x, pltpu.HBM)
        for x in (embeddings, frame_weight.reshape(4, 128), candidates.reshape(4, count), owner)
    ))
    out, best = pl.pallas_call(
        settle,
        out_shape=(
            jax.ShapeDtypeStruct(out.shape, out.dtype),
            jax.ShapeDtypeStruct(best.shape, best.dtype),
        ),
        in_specs=[vmem, vmem],
        out_specs=(hbm, hbm),
        scratch_shapes=[dma((2,))],
        name="settle",
    )(*(pltpu.with_memory_space_constraint(x, pltpu.VMEM) for x in (out, best)))
    return best.reshape(F), out.reshape(1, 1, GROUPS, CAP, PIECE, PIECE)


def solution(mesh):
    return jax.shard_map(
        functools.partial(body, mesh.shape["blk"]),
        mesh=mesh,
        in_specs=(P(("blk", "grp"), None), P(("blk", "grp")), P("blk", "grp", None, None), P()),
        out_specs=(P(("blk", "grp")), P("blk", "grp", None, None, None, None)),
        check_vma=False,
    )
```
